32 devices in a mesh: row: 16 (over z, y, x), col: 2 (over core).
Axes of the slice: x: 2, y: 2, z: 4, core: 2. Of those that a mesh axis runs over, the one named last changes fastest.
Arguments:
- tensor: float32 [8, 2048, 2048], P(None, 'row', 'col'), may hold values from -0.8 to 0.8
- factor_a: float32 [2048, 256], P(('row', 'col')), may hold values from -0.125 to 0.125
- factor_bt: float32 [256, 2048], P('row', 'col'), may hold values from -0.125 to 0.125
- factor_c: float32 [8, 256], replicated, may hold values from -6 to 6
Outputs:
- grad_a: float32 [2048, 256], P(('row', 'col'))
- grad_bt: float32 [256, 2048], P('row', 'col')
- grad_c: float32 [8, 256], replicated
The draws below stay inside these ranges and needn't reach their ends.
All inputs are finite; a program needn't handle non-finite values.
Results may differ from the reference program's by a relative error of at most 0.0001.
Values sent between devices are 32-bit elements; how exact they have to be, the bound alone decides.
No kernel may reach another device: no remote copies, remote signals or barrier semaphores. Data moves between devices by JAX's collectives and lax.ppermute only.
A program may use at most 64 MiB of HBM per device.

```python
import jax
import jax.numpy as jnp
from jax import lax

R = 256
K = 8
I = 2048
J = 2048


def steps_of(rng, shape, shards, low, largest):
    def one(axis_at, parts):
        steps = jax.random.uniform(jax.random.fold_in(jax.random.fold_in(rng, 6), axis_at), (parts,), jnp.float32, low / len(shards), largest / len(shards))
        return jnp.repeat(jnp.exp(steps), shape[axis_at] // parts).reshape((-1,) + (1,) * (len(shape) - axis_at - 1))

    gain = one(*shards[0])
    for cut in shards[1:]:
        gain = gain * one(*cut)
    return gain


def bell_draw(own_key, dims, deviation, bound, pieces=(), held_as=jnp.bfloat16):
    array = deviation * jax.random.normal(own_key, dims, jnp.float32)
    if pieces:
        array = array * steps_of(own_key, dims, pieces, -0.22, 0.18)
    return jnp.clip(array, -bound, bound).astype(held_as)


def setup_inputs(seed: int = 0) -> dict:
    key_list = jax.random.split(jax.random.key(seed), 5)
    tensor = bell_draw(key_list[0], (K, I, J), 0.1, 0.8, ((1, 16), (2, 2)), jnp.float32)
    factor_a = bell_draw(key_list[1], (I, R), I ** -0.5, 0.125, ((0, 32),), jnp.float32)
    factor_bt = bell_draw(key_list[2], (R, J), J ** -0.5, 0.125, ((0, 16), (1, 2)), jnp.float32)
    factor_c = bell_draw(key_list[3], (K, R), 1.0, 6.0, (), jnp.float32)
    return {"tensor": tensor, "factor_a": factor_a, "factor_bt": factor_bt, "factor_c": factor_c}


def reference(tensor, factor_a, factor_bt, factor_c):
    highest = lax.Precision.HIGHEST
    gram_a = jnp.dot(factor_a.T, factor_a, precision=highest)
    gram_b = jnp.dot(factor_bt, factor_bt.T, precision=highest)
    gram_c = jnp.dot(factor_c.T, factor_c, precision=highest)

    def slice_step(carry, inputs):
        sum_a, sum_bt = carry
        slab, c_row = inputs
        contracted = jnp.dot(slab, factor_bt.T, precision=highest)
        sum_a = sum_a + c_row[None, :] * contracted
        c_term = jnp.sum(factor_a * contracted, axis=0)
        sum_bt = sum_bt + jnp.dot((factor_a * c_row[None, :]).T, slab, precision=highest)
        return (sum_a, sum_bt), c_term

    start_a = jnp.zeros(factor_a.shape, factor_a.dtype)
    start_bt = jnp.zeros(factor_bt.shape, factor_bt.dtype)
    (mttkrp_a, mttkrp_bt), mttkrp_c = lax.scan(slice_step, (start_a, start_bt), (tensor, factor_c))
    grad_a = jnp.dot(factor_a, gram_b * gram_c, precision=highest) - mttkrp_a
    grad_bt = jnp.dot(gram_a * gram_c, factor_bt, precision=highest) - mttkrp_bt
    grad_c = jnp.dot(factor_c, gram_a * gram_b, precision=highest) - mttkrp_c
    return grad_a, grad_bt, grad_c
```

```python
import functools

import jax
import jax.numpy as jnp
from jax import lax
from jax.experimental import pallas as pl
from jax.experimental.pallas import tpu as pltpu
from jax.sharding import PartitionSpec as P

F32 = jnp.float32
BF16 = jnp.bfloat16
NN = (((1,), (0,)), ((), ()))
NT = (((1,), (1,)), ((), ()))
VMEM = 24 * 1024 * 1024
EARLY_VMEM = VMEM
AHEAD = 4


def split(x):
    high = x.astype(BF16)
    return high, (x - high.astype(F32)).astype(BF16)


def dot3(a, b, dims=NN):
    mul = functools.partial(lax.dot_general, dimension_numbers=dims, preferred_element_type=F32)
    return mul(a[0], b[0]) + (mul(a[0], b[1]) + mul(a[1], b[0]))


def hop(stage, stages, parity):
    return 1 << (stage + (1 - parity) * (stages - 1 - 2 * stage))


def distance(slot, n_line, parity):
    stages = n_line.bit_length() - 1
    return sum(hop(t, stages, parity) for t in range(stages) if slot >> t & 1)


def block_rows(n_line, rank_rows):
    row, col = lax.axis_index("row"), lax.axis_index("col")
    line, spot, parity = row // 4, row % 4, col % 2
    step = 1 + parity
    places = (spot, spot ^ step, spot ^ (3 - step), spot ^ 3)
    return [
        [
            pl.multiple_of((4 * (line ^ distance(d, n_line, parity)) + place) * rank_rows, rank_rows)
            for d in range(n_line)
        ]
        for place in places
    ]


def early_kernel(n_line, rank_rows, width, t_hbm, a_hbm, c_hbm, own_hbm, other_ref, *refs):
    *pay, slab_ref, high_ref, low_ref, gram_ref, block_ref, c_ref, own_ref, total, t_ref, a_ref, wide, sems = refs
    slices, rows, cols = t_hbm.shape
    group = slices // 2
    steps = slices // group

    def load(k):
        part = pl.ds(k * group, group)
        return pltpu.make_async_copy(t_hbm.at[part], t_ref.at[part], sems.at[k])

    first = [
        pltpu.make_async_copy(a_hbm, a_ref, sems.at[slices]),
        pltpu.make_async_copy(c_hbm, c_ref, sems.at[slices + 1]),
    ]
    last = pltpu.make_async_copy(own_hbm, own_ref, sems.at[slices + 2])
    for copy in first + [load(k) for k in range(min(AHEAD, steps))] + [last]:
        copy.start()
    for copy in first:
        copy.wait()
    if other_ref is None:
        block_ref[...] = a_ref[...]
    else:
        here = lax.axis_index("col") == 0
        half = rows // 2
        block_ref[:half, :] = jnp.where(here, a_ref[...], other_ref[...])
        block_ref[half:, :] = jnp.where(here, other_ref[...], a_ref[...])
    rank = block_ref.shape[1]
    a = block_ref[...]
    a_t = a.T
    c_t = c_ref[...].T
    for k in range(slices):
        wide[k] = jnp.broadcast_to(c_t[:, k : k + 1], wide.shape[1:])
    a_pair = split(a_t)
    both = jnp.concatenate(a_pair, axis=1)
    gram = dot3(a_pair, split(a))
    gram_ref[...] = gram
    total[:, :cols] = jnp.zeros((rank, cols), F32)
    if width == rank:
        total[:, cols:] = gram
    else:
        mine = lax.axis_index("col")
        for part in range(rank // width):

            @pl.when(mine == part)
            def _():
                total[:, cols:] = gram[:, part * width : (part + 1) * width]

    @pl.loop(0, steps)
    def _(step):
        load(step).wait()

        @pl.when(step + AHEAD < steps)
        def _():
            load(step + AHEAD).start()

        mul = functools.partial(jnp.dot, preferred_element_type=F32)
        slabs, scales = [], []
        for i in range(group):
            k = step * group + i
            high, low = split(t_ref[k])
            here = pl.ds(pl.multiple_of(k * rows, rows), rows)
            high_ref[here, :] = high
            low_ref[here, :] = low
            slab = mul(both, jnp.concatenate([high, high], axis=0)) + mul(
                both, jnp.concatenate([low, low], axis=0)
            )
            slab_ref[k] = slab
            slabs.append(slab)
            scales.append(wide[k])
        lanes = wide.shape[2]
        for at in range(0, cols, lanes):
            total[:, at : at + lanes] += sum(
                scale * slab[:, at : at + lanes] for scale, slab in zip(scales, slabs)
            )

    last.wait()
    if len(pay) == 1:
        pay[0][...] = total[...]
    else:
        for ref, starts in zip(pay, block_rows(n_line, rank_rows)):
            for d, start in enumerate(starts):
                ref[d * rank_rows : (d + 1) * rank_rows, :] = total[pl.ds(start, rank_rows), :]


def ranks_kernel(n_line, rank_rows, slab_ref, c_ref, gram_ref, *refs):
    *bufs, high_ref, low_ref, cross_ref, out_ref, bt_ref = refs
    if len(bufs) == 1:
        bt_ref[...] = bufs[0][...]
    else:
        own, near, far = bufs
        line_rows = n_line * rank_rows
        at = [(own, 0), (near, 0), (far, 0), (far, line_rows)]
        for (ref, base), starts in zip(at, block_rows(n_line, rank_rows)):
            for d, start in enumerate(starts):
                bt_ref[pl.ds(start, rank_rows), :] = ref[base + d * rank_rows : base + (d + 1) * rank_rows, :]
    bt = split(bt_ref[...])
    high_ref[...], low_ref[...] = bt
    cross = dot3(bt, bt, NT)
    cross_ref[...] = cross
    slices, rank = c_ref.shape
    sums = [
        jnp.sum(slab_ref[k] * bt_ref[...], axis=1, keepdims=True) for k in range(slices)
    ]
    sums = jnp.concatenate(sums, axis=1)
    out_ref[...] = dot3(split(c_ref[...]), split(gram_ref[...] * cross)) - sums.T


def rows_kernel(halves, high_ref, low_ref, bt_high, bt_low, a_ref, c_ref, cross_ref, keep_ref, send_ref=None):
    rows, rank = a_ref.shape
    slices = c_ref.shape[0]
    bt = (bt_high[...], bt_low[...])
    total = None
    for k in range(0, slices, 2):
        here = pl.ds(k * rows, 2 * rows)
        contracted = dot3((high_ref[here, :], low_ref[here, :]), bt, NT)
        part = c_ref[k : k + 1, :] * contracted[:rows] + c_ref[k + 1 : k + 2, :] * contracted[rows:]
        total = part if total is None else total + part
    gram_c = dot3(split(c_ref[...].T), split(c_ref[...]))
    grad = dot3(split(a_ref[...]), split(cross_ref[...] * gram_c)) - total
    if not halves:
        keep_ref[...] = grad
        return
    half = rows // 2
    mine = lax.axis_index("col")

    @pl.when(mine == 0)
    def _():
        keep_ref[...] = grad[:half]
        send_ref[...] = grad[half:]

    @pl.when(mine == 1)
    def _():
        keep_ref[...] = grad[half:]
        send_ref[...] = grad[:half]


def last_kernel(mine_ref, other_ref, c_ref, m_ref, high_ref, low_ref, out_ref):
    rank_rows = m_ref.shape[0]
    pieces = [mine_ref[...]]
    if other_ref is not None:
        here = lax.axis_index("col") == 0
        pieces = [
            jnp.where(here, mine_ref[...], other_ref[...]),
            jnp.where(here, other_ref[...], mine_ref[...]),
        ]
    gram_rows = jnp.concatenate(pieces, axis=1)
    c = c_ref[...]
    chosen = lax.axis_index("row") * rank_rows
    rank = c.shape[1]
    pick = lax.broadcasted_iota(jnp.int32, (rank_rows, rank), 1) == (
        chosen + lax.broadcasted_iota(jnp.int32, (rank_rows, rank), 0)
    )
    exact = functools.partial(
        lax.dot_general, precision=lax.Precision.HIGHEST, preferred_element_type=F32
    )
    c_mine = exact(pick.astype(F32), c, NT)
    h_rows = gram_rows * exact(c_mine, c, NN)
    out_ref[...] = dot3(split(h_rows), (high_ref[...], low_ref[...])) - m_ref[...]


def local(n_row, n_col, tensor, factor_a, factor_bt, factor_c):
    slices, rows, cols = tensor.shape
    rank_rows, rank = factor_bt.shape[0], factor_c.shape[1]
    n_line = n_row // 4
    line_rows = n_line * rank_rows
    inside = rank_rows % 16 == 0
    pair = n_col == 2
    width = rank // n_col if (rank // n_col) % 128 == 0 and pair else rank

    def move(x, target):
        return lax.ppermute(
            x,
            ("row", "col"),
            [(r * n_col + c, target(r, c) * n_col + c) for r in range(n_row) for c in range(n_col)],
        )

    def swap(x):
        return lax.ppermute(x, "col", [(0, 1), (1, 0)])

    first = lambda r, c: r ^ (1 + c % 2)
    second = lambda r, c: r ^ (2 - c % 2)

    stages = n_line.bit_length() - 1

    def along(t):
        return lambda r, c: r ^ (4 * hop(t, stages, c % 2))

    def call(kernel, name, cost, shapes, scratch=()):
        return pl.pallas_call(
            kernel,
            out_shape=[jax.ShapeDtypeStruct(*x) for x in shapes],
            scratch_shapes=[pltpu.VMEM(x, F32) for x in scratch],
            compiler_params=pltpu.CompilerParams(vmem_limit_bytes=VMEM),
            cost_estimate=pl.CostEstimate(flops=cost, bytes_accessed=0, transcendentals=0),
            name=name,
        )

    tie = lax.optimization_barrier

    if pair:
        a_parts = [factor_a, swap(factor_a)]
    else:
        a_parts = [lax.all_gather(factor_a, "col", axis=0, tiled=True)]
    got = move(factor_bt, along(0))

    work = 2 * slices * rows * cols * rank
    pay_rows = [line_rows] * 4 if inside else [rank]
    early = functools.partial(early_kernel, n_line, rank_rows, width)
    if pair:
        kernel = early
    else:
        kernel = lambda t_ref, a_ref, c_ref, b_ref, *refs: early(t_ref, a_ref, c_ref, b_ref, None, *refs)
    fixed = pltpu.with_memory_space_constraint
    hbm = pl.BlockSpec(memory_space=pltpu.HBM)
    vmem = pl.BlockSpec(memory_space=pltpu.VMEM)
    *pay, slabs, high, low, gram, block_a, c_near, own = pl.pallas_call(
        kernel,
        in_specs=[hbm] * 4 + [vmem] * (len(a_parts) - 1),
        out_shape=[jax.ShapeDtypeStruct((n, cols + width), F32) for n in pay_rows]
        + [jax.ShapeDtypeStruct((slices, rank, cols), F32)]
        + [jax.ShapeDtypeStruct((slices * rows, cols), BF16)] * 2
        + [jax.ShapeDtypeStruct(x, F32) for x in ((rank, rank), (rows, rank), (slices, rank), factor_bt.shape)],
        scratch_shapes=[
            pltpu.VMEM((rank, cols + width), F32),
            pltpu.VMEM((slices, rows, cols), F32),
            pltpu.VMEM(a_parts[0].shape, F32),
            pltpu.VMEM((slices, rank, 128), F32),
            pltpu.SemaphoreType.DMA((slices + 3,)),
        ],
        compiler_params=pltpu.CompilerParams(vmem_limit_bytes=EARLY_VMEM),
        cost_estimate=pl.CostEstimate(flops=work, bytes_accessed=0, transcendentals=0),
        name="early",
    )(*(fixed(x, pltpu.HBM) for x in (tensor, a_parts[0], factor_c, factor_bt)), *a_parts[1:])
    if not inside:
        row, parity = lax.axis_index("row"), lax.axis_index("col") % 2
        line, spot, step = row // 4, row % 4, 1 + parity
        lines = jnp.stack([line ^ distance(d, n_line, parity) for d in range(n_line)])
        places = (spot, spot ^ step, spot ^ (3 - step), spot ^ 3)
        blocks = pay[0].reshape(n_line, 4, rank_rows, cols + width)
        pay = [
            jnp.take(jnp.take(blocks, place, axis=1), lines, axis=0).reshape(line_rows, cols + width)
            for place in places
        ]
    pay_own, pay_f, pay_s, pay_fs = pay
    pay_fs, pay_f, got = tie((pay_fs, pay_f, got))
    got_fs = move(pay_fs, first)
    got_f = move(pay_f, first)

    own4 = jnp.concatenate([own, got], axis=0)
    for t in range(1, stages):
        own4 = jnp.concatenate([own4, move(own4, along(t))], axis=0)
    own4, got_fs = tie((own4, got_fs))
    f4 = move(own4, first)
    f4, got_f = tie((f4, got_f))
    far4 = move(jnp.concatenate([own4, f4], axis=0), second)

    got_s = move(pay_s + got_fs, second)
    total = pay_own + got_f + got_s
    bufs = [own4, f4, far4]
    if not inside:
        table = jnp.concatenate(bufs, axis=0).reshape(n_row, rank_rows, cols)
        index = jnp.argsort(jnp.concatenate([4 * lines + place for place in places]))
        bufs = [jnp.take(table, index, axis=0).reshape(rank, cols)]
    bt_high, bt_low, cross, part_c = call(
        functools.partial(ranks_kernel, n_line, rank_rows),
        "ranks",
        2 * cols * rank * rank,
        [((rank, cols), BF16)] * 2 + [((rank, rank), F32), ((slices, rank), F32)],
        [(rank, cols)],
    )(slabs, c_near, gram, *bufs)

    part_c = part_c + move(part_c, second)
    slots = jnp.split(total, n_line, axis=0)
    total = slots[0]
    for d in range(1, n_line):
        total = total + move(slots[d], lambda r, c, d=d: r ^ (4 * distance(d, n_line, c % 2)))

    half = rows // 2 if pair else rows
    keep, *send = call(
        functools.partial(rows_kernel, pair),
        "rows",
        work,
        [((half, rank), F32)] * (2 if pair else 1),
    )(high, low, bt_high, bt_low, block_a, c_near, cross)

    gram_rows = total[:, cols:]
    kernel = last_kernel
    operands = [gram_rows, c_near, total[:, :cols], bt_high, bt_low]
    if width < rank:
        operands.insert(1, swap(gram_rows))
    else:
        kernel = lambda first_ref, *refs: last_kernel(first_ref, None, *refs)
    (grad_bt,) = call(kernel, "last", 2 * rank_rows * cols * rank, [((rank_rows, cols), F32)])(*operands)

    part_c = part_c + move(part_c, first)
    part_c, keep, send = tie((part_c, keep, send))
    spread = [move(part_c, lambda r, c, d=d: r ^ (4 * d)) for d in [*range(2, n_line), 1]]
    for x in spread:
        part_c = part_c + x
    part_c, grad_bt = tie((part_c, grad_bt))
    if pair:
        grad_a = keep + swap(send[0])
        grad_c = part_c + swap(part_c)
    else:
        grad_a = lax.psum_scatter(keep, "col", scatter_dimension=0, tiled=True)
        grad_c = lax.psum(part_c, "col")
    return grad_a, grad_bt, grad_c


def solution(mesh):
    in_specs = (P(None, "row", "col"), P(("row", "col"), None), P("row", "col"), P())
    out_specs = (P(("row", "col"), None), P("row", "col"), P())
    body = functools.partial(local, mesh.shape["row"], mesh.shape["col"])
    return jax.shard_map(body, mesh=mesh, in_specs=in_specs, out_specs=out_specs, check_vma=False)
```

```python
import functools

import jax
import jax.numpy as jnp
from jax import lax
from jax.experimental import pallas as pl
from jax.experimental.pallas import tpu as pltpu
from jax.sharding import PartitionSpec as P

F32 = jnp.float32
BF16 = jnp.bfloat16
NN = (((1,), (0,)), ((), ()))
NT = (((1,), (1,)), ((), ()))
VMEM = 24 * 1024 * 1024
EARLY_VMEM = VMEM
AHEAD = 4
WEIGHT = 200


def split(x):
    high = x.astype(BF16)
    return high, (x - high.astype(F32)).astype(BF16)


def dot3(a, b, dims=NN):
    mul = functools.partial(lax.dot_general, dimension_numbers=dims, preferred_element_type=F32)
    return mul(a[0], b[0]) + (mul(a[0], b[1]) + mul(a[1], b[0]))


def hop(stage, stages, parity):
    return 1 << (stage + (1 - parity) * (stages - 1 - 2 * stage))


def distance(slot, n_line, parity):
    stages = n_line.bit_length() - 1
    return sum(hop(t, stages, parity) for t in range(stages) if slot >> t & 1)


def block_rows(n_line, rank_rows):
    row, col = lax.axis_index("row"), lax.axis_index("col")
    line, spot, parity = row // 4, row % 4, col % 2
    step = 1 + parity
    places = (spot, spot ^ step, spot ^ (3 - step), spot ^ 3)
    return [
        [
            pl.multiple_of((4 * (line ^ distance(d, n_line, parity)) + place) * rank_rows, rank_rows)
            for d in range(n_line)
        ]
        for place in places
    ]


def early_kernel(n_line, rank_rows, width, t_hbm, a_hbm, c_hbm, own_hbm, other_ref, *refs):
    *pay, slab_ref, high_ref, low_ref, gram_ref, block_ref, c_ref, own_ref, total, t_ref, a_ref, wide, sems = refs
    slices, rows, cols = t_hbm.shape
    group = slices // 2
    steps = slices // group

    def load(k):
        part = pl.ds(k * group, group)
        return pltpu.make_async_copy(t_hbm.at[part], t_ref.at[part], sems.at[k])

    first = [
        pltpu.make_async_copy(a_hbm, a_ref, sems.at[slices]),
        pltpu.make_async_copy(c_hbm, c_ref, sems.at[slices + 1]),
    ]
    last = pltpu.make_async_copy(own_hbm, own_ref, sems.at[slices + 2])
    for copy in first + [load(k) for k in range(min(AHEAD, steps))] + [last]:
        copy.start()
    for copy in first:
        copy.wait()
    if other_ref is None:
        block_ref[...] = a_ref[...]
    else:
        here = lax.axis_index("col") == 0
        half = rows // 2
        block_ref[:half, :] = jnp.where(here, a_ref[...], other_ref[...])
        block_ref[half:, :] = jnp.where(here, other_ref[...], a_ref[...])
    rank = block_ref.shape[1]
    a = block_ref[...]
    a_t = a.T
    c_t = c_ref[...].T
    for k in range(slices):
        wide[k] = jnp.broadcast_to(c_t[:, k : k + 1], wide.shape[1:])
    a_pair = split(a_t)
    both = jnp.concatenate(a_pair, axis=1)
    gram = dot3(a_pair, split(a))
    gram_ref[...] = gram
    total[:, :cols] = jnp.zeros((rank, cols), F32)
    if width == rank:
        total[:, cols:] = gram
    else:
        mine = lax.axis_index("col")
        for part in range(rank // width):

            @pl.when(mine == part)
            def _():
                total[:, cols:] = gram[:, part * width : (part + 1) * width]

    @pl.loop(0, steps)
    def _(step):
        load(step).wait()

        @pl.when(step + AHEAD < steps)
        def _():
            load(step + AHEAD).start()

        mul = functools.partial(jnp.dot, preferred_element_type=F32)
        slabs, scales = [], []
        for i in range(group):
            k = step * group + i
            high, low = split(t_ref[k])
            here = pl.ds(pl.multiple_of(k * rows, rows), rows)
            high_ref[here, :] = high
            low_ref[here, :] = low
            slab = mul(both, jnp.concatenate([high, high], axis=0)) + mul(
                both, jnp.concatenate([low, low], axis=0)
            )
            slab_ref[k] = slab
            slabs.append(slab)
            scales.append(wide[k])
        lanes = wide.shape[2]
        for at in range(0, cols, lanes):
            total[:, at : at + lanes] += sum(
                scale * slab[:, at : at + lanes] for scale, slab in zip(scales, slabs)
            )

    last.wait()
    if len(pay) == 1:
        pay[0][...] = total[...]
    else:
        for ref, starts in zip(pay, block_rows(n_line, rank_rows)):
            for d, start in enumerate(starts):
                ref[d * rank_rows : (d + 1) * rank_rows, :] = total[pl.ds(start, rank_rows), :]


def put_ranks(slab_ref, ref, starts, count, high_ref, low_ref, sums_ref):
    for d, start in enumerate(starts):
        block = ref[d * count : (d + 1) * count, :]
        here = pl.ds(start, count)
        high_ref[here, :], low_ref[here, :] = split(block)
        sums_ref[here, :] = jnp.concatenate(
            [
                jnp.sum(slab_ref[k, here, :] * block, axis=1, keepdims=True)
                for k in range(slab_ref.shape[0])
            ],
            axis=1,
        )


def near_kernel(n_line, rank_rows, slab_ref, *refs):
    *bufs, high_ref, low_ref, sums_ref = refs
    for ref, starts in zip(bufs, block_rows(n_line, rank_rows)):
        put_ranks(slab_ref, ref, starts, rank_rows, high_ref, low_ref, sums_ref)


def ranks_kernel(n_line, rank_rows, slab_ref, c_ref, gram_ref, buf_ref, *refs):
    *sofar, high_ref, low_ref, cross_ref, out_ref, sums_ref = refs
    if sofar:
        for ref, out in zip(sofar, (high_ref, low_ref, sums_ref)):
            out[...] = ref[...]
        starts, count = block_rows(n_line, rank_rows)[3], rank_rows
    else:
        starts, count = [0], buf_ref.shape[0]
    put_ranks(slab_ref, buf_ref, starts, count, high_ref, low_ref, sums_ref)
    bt = (high_ref[...], low_ref[...])
    cross = dot3(bt, bt, NT)
    cross_ref[...] = cross
    out_ref[...] = dot3(split(c_ref[...]), split(gram_ref[...] * cross)) - sums_ref[...].T


def rows_kernel(halves, high_ref, low_ref, bt_high, bt_low, a_ref, c_ref, cross_ref, keep_ref, send_ref=None):
    rows, rank = a_ref.shape
    slices = c_ref.shape[0]
    bt = (bt_high[...], bt_low[...])
    total = None
    for k in range(0, slices, 2):
        here = pl.ds(k * rows, 2 * rows)
        contracted = dot3((high_ref[here, :], low_ref[here, :]), bt, NT)
        part = c_ref[k : k + 1, :] * contracted[:rows] + c_ref[k + 1 : k + 2, :] * contracted[rows:]
        total = part if total is None else total + part
    gram_c = dot3(split(c_ref[...].T), split(c_ref[...]))
    grad = dot3(split(a_ref[...]), split(cross_ref[...] * gram_c)) - total
    if not halves:
        keep_ref[...] = grad
        return
    half = rows // 2
    mine = lax.axis_index("col")

    @pl.when(mine == 0)
    def _():
        keep_ref[...] = grad[:half]
        send_ref[...] = grad[half:]

    @pl.when(mine == 1)
    def _():
        keep_ref[...] = grad[half:]
        send_ref[...] = grad[:half]


def sum_kernel(a_ref, b_ref, out_ref):
    out_ref[...] = a_ref[...] + b_ref[...]


def last_kernel(pair, halves, *refs):
    gram_refs, refs = refs[: 1 + halves], refs[1 + halves :]
    c_ref, m_ref, high_ref, low_ref, *refs = refs
    if pair:
        keep_ref, back_ref, *parts, out_ref, a_out, c_out = refs
        a_out[...] = keep_ref[...] + back_ref[...]
        c_out[...] = sum(ref[...] for ref in parts[1:]) + parts[0][...]
    else:
        (out_ref,) = refs
    rank_rows = m_ref.shape[0]
    pieces = [ref[...] for ref in gram_refs]
    if halves:
        here = lax.axis_index("col") == 0
        pieces = [jnp.where(here, *pieces), jnp.where(here, *pieces[::-1])]
    gram_rows = jnp.concatenate(pieces, axis=1)
    c = c_ref[...]
    chosen = lax.axis_index("row") * rank_rows
    rank = c.shape[1]
    pick = lax.broadcasted_iota(jnp.int32, (rank_rows, rank), 1) == (
        chosen + lax.broadcasted_iota(jnp.int32, (rank_rows, rank), 0)
    )
    exact = functools.partial(
        lax.dot_general, precision=lax.Precision.HIGHEST, preferred_element_type=F32
    )
    c_mine = exact(pick.astype(F32), c, NT)
    h_rows = gram_rows * exact(c_mine, c, NN)
    out_ref[...] = dot3(split(h_rows), (high_ref[...], low_ref[...])) - m_ref[...]


def local(n_row, n_col, tensor, factor_a, factor_bt, factor_c):
    slices, rows, cols = tensor.shape
    rank_rows, rank = factor_bt.shape[0], factor_c.shape[1]
    n_line = n_row // 4
    line_rows = n_line * rank_rows
    inside = rank_rows % 16 == 0
    pair = n_col == 2
    width = rank // n_col if (rank // n_col) % 128 == 0 and pair else rank

    def move(x, target):
        return lax.ppermute(
            x,
            ("row", "col"),
            [(r * n_col + c, target(r, c) * n_col + c) for r in range(n_row) for c in range(n_col)],
        )

    def swap(x):
        return lax.ppermute(x, "col", [(0, 1), (1, 0)])

    first = lambda r, c: r ^ (1 + c % 2)
    second = lambda r, c: r ^ (2 - c % 2)

    stages = n_line.bit_length() - 1

    def along(t):
        return lambda r, c: r ^ (4 * hop(t, stages, c % 2))

    def call(kernel, name, cost, shapes, scratch=()):
        return pl.pallas_call(
            kernel,
            out_shape=[jax.ShapeDtypeStruct(*x) for x in shapes],
            scratch_shapes=[pltpu.VMEM(x, F32) for x in scratch],
            compiler_params=pltpu.CompilerParams(vmem_limit_bytes=VMEM),
            cost_estimate=pl.CostEstimate(flops=cost, bytes_accessed=0, transcendentals=0),
            name=name,
        )

    tie = lax.optimization_barrier

    if pair:
        a_parts = [factor_a, swap(factor_a)]
    else:
        a_parts = [lax.all_gather(factor_a, "col", axis=0, tiled=True)]
    apart = [lambda r, c, d=d: r ^ (4 * distance(d, n_line, c % 2)) for d in range(n_line)]
    got = [move(factor_bt, apart[d]) for d in range(1, n_line)]

    work = 2 * slices * rows * cols * rank
    pay_rows = [line_rows] * 4 if inside else [rank]
    early = functools.partial(early_kernel, n_line, rank_rows, width)
    if pair:
        kernel = early
    else:
        kernel = lambda t_ref, a_ref, c_ref, b_ref, *refs: early(t_ref, a_ref, c_ref, b_ref, None, *refs)
    fixed = pltpu.with_memory_space_constraint
    hbm = pl.BlockSpec(memory_space=pltpu.HBM)
    vmem = pl.BlockSpec(memory_space=pltpu.VMEM)
    *pay, slabs, high, low, gram, block_a, c_near, own = pl.pallas_call(
        kernel,
        in_specs=[hbm] * 4 + [vmem] * (len(a_parts) - 1),
        out_shape=[jax.ShapeDtypeStruct((n, cols + width), F32) for n in pay_rows]
        + [jax.ShapeDtypeStruct((slices, rank, cols), F32)]
        + [jax.ShapeDtypeStruct((slices * rows, cols), BF16)] * 2
        + [jax.ShapeDtypeStruct(x, F32) for x in ((rank, rank), (rows, rank), (slices, rank), factor_bt.shape)],
        scratch_shapes=[
            pltpu.VMEM((rank, cols + width), F32),
            pltpu.VMEM((slices, rows, cols), F32),
            pltpu.VMEM(a_parts[0].shape, F32),
            pltpu.VMEM((slices, rank, 128), F32),
            pltpu.SemaphoreType.DMA((slices + 3,)),
        ],
        compiler_params=pltpu.CompilerParams(vmem_limit_bytes=EARLY_VMEM),
        cost_estimate=pl.CostEstimate(flops=work, bytes_accessed=0, transcendentals=0),
        name="early",
    )(*(fixed(x, pltpu.HBM) for x in (tensor, a_parts[0], factor_c, factor_bt)), *a_parts[1:])
    if not inside:
        row, parity = lax.axis_index("row"), lax.axis_index("col") % 2
        line, spot, step = row // 4, row % 4, 1 + parity
        lines = jnp.stack([line ^ distance(d, n_line, parity) for d in range(n_line)])
        places = (spot, spot ^ step, spot ^ (3 - step), spot ^ 3)
        blocks = pay[0].reshape(n_line, 4, rank_rows, cols + width)
        pay = [
            jnp.take(jnp.take(blocks, place, axis=1), lines, axis=0).reshape(line_rows, cols + width)
            for place in places
        ]
    pay_own, pay_f, pay_s, pay_fs = pay
    got_f = move(pay_f, first)
    got_fs = move(pay_fs, first)

    own4 = jnp.concatenate([own, *got], axis=0)
    f4 = move(own4, first)
    s4 = move(own4, second)
    f4, s4 = tie((f4, s4))
    fs4 = move(f4, second)
    if inside:
        sofar = call(
            functools.partial(near_kernel, n_line, rank_rows),
            "near",
            WEIGHT * cols * rank * rank,
            [((rank, cols), BF16)] * 2 + [((rank, slices), F32)],
        )(slabs, own4, f4, s4)
        got_fs, _ = tie((got_fs, sofar[2]))
        last_ranks = fs4
    else:
        sofar = []
        table = jnp.concatenate([own4, f4, s4, fs4], axis=0).reshape(n_row, rank_rows, cols)
        index = jnp.argsort(jnp.concatenate([4 * lines + place for place in places]))
        last_ranks = jnp.take(table, index, axis=0).reshape(rank, cols)
    bt_high, bt_low, cross, part_c = call(
        functools.partial(ranks_kernel, n_line, rank_rows),
        "ranks",
        WEIGHT * cols * rank * rank,
        [((rank, cols), BF16)] * 2 + [((rank, rank), F32), ((slices, rank), F32)],
        [(rank, slices)],
    )(slabs, c_near, gram, last_ranks, *sofar)

    got_s = move(pay_s + got_fs, second)

    (mark,) = call(sum_kernel, "mark", WEIGHT * work, [(part_c.shape, F32)])(part_c, part_c)
    part_c = part_c + swap(part_c) if pair else lax.psum(part_c, "col")
    (part_c,) = call(sum_kernel, "sum", WEIGHT * work, [(part_c.shape, F32)])(part_c, move(part_c, second))
    pay_own, _ = tie((pay_own, mark))
    total = pay_own + got_f + got_s
    slots = jnp.split(total, n_line, axis=0)
    total = slots[0]
    for d in range(1, n_line):
        total = total + move(slots[d], apart[d])
    cross, _ = tie((cross, part_c))
    part_c = part_c + move(part_c, first)

    half = rows // 2 if pair else rows
    keep, *send = call(
        functools.partial(rows_kernel, pair),
        "rows",
        work,
        [((half, rank), F32)] * (2 if pair else 1),
    )(high, low, bt_high, bt_low, block_a, c_near, cross)

    part_c = [part_c] + [move(part_c, lambda r, c, d=d: r ^ (4 * d)) for d in reversed(range(1, n_line))]
    gram_rows = total[:, cols:]
    grams = [gram_rows, swap(gram_rows)] if width < rank else [gram_rows]
    operands = [*grams, c_near, total[:, :cols], bt_high, bt_low]
    shapes = [((rank_rows, cols), F32)]
    if pair:
        operands += [keep, swap(send[0]), *part_c]
        shapes += [(keep.shape, F32), (factor_c.shape, F32)]
    grad_bt, *rest = call(
        functools.partial(last_kernel, pair, len(grams) - 1), "last", rank_rows * cols * rank, shapes
    )(*operands)
    if pair:
        return rest[0], grad_bt, rest[1]
    grad_a = lax.psum_scatter(keep, "col", scatter_dimension=0, tiled=True)
    return grad_a, grad_bt, sum(part_c[1:], part_c[0])


def solution(mesh):
    in_specs = (P(None, "row", "col"), P(("row", "col"), None), P("row", "col"), P())
    out_specs = (P(("row", "col"), None), P("row", "col"), P())
    body = functools.partial(local, mesh.shape["row"], mesh.shape["col"])
    return jax.shard_map(body, mesh=mesh, in_specs=in_specs, out_specs=out_specs, check_vma=False)
```

```python
import functools

import jax
import jax.numpy as jnp
from jax import lax
from jax.experimental import pallas as pl
from jax.experimental.pallas import tpu as pltpu
from jax.sharding import PartitionSpec as P

F32 = jnp.float32
BF16 = jnp.bfloat16
NN = (((1,), (0,)), ((), ()))
NT = (((1,), (1,)), ((), ()))
VMEM = 24 * 1024 * 1024
EARLY_VMEM = VMEM
AHEAD = 4
WEIGHT = 200


def split(x):
    high = x.astype(BF16)
    return high, (x - high.astype(F32)).astype(BF16)


def dot3(a, b, dims=NN):
    mul = functools.partial(lax.dot_general, dimension_numbers=dims, preferred_element_type=F32)
    return mul(a[0], b[0]) + (mul(a[0], b[1]) + mul(a[1], b[0]))


def distance(slot, n_line, parity):
    if slot in (0, n_line - 1):
        return min(slot, 1)
    return (slot + 1) ^ parity


def block_rows(n_line, rank_rows):
    row, col = lax.axis_index("row"), lax.axis_index("col")
    line, spot, parity = row // 4, row % 4, col % 2
    step = 1 + parity
    places = (spot, spot ^ step, spot ^ (3 - step), spot ^ 3)
    return [
        [
            pl.multiple_of((4 * (line ^ distance(d, n_line, parity)) + place) * rank_rows, rank_rows)
            for d in range(n_line)
        ]
        for place in places
    ]


def early_kernel(n_line, rank_rows, width, t_hbm, a_hbm, c_hbm, own_hbm, other_ref, *refs):
    *pay, slab_ref, high_ref, low_ref, gram_ref, block_ref, c_ref, own_ref, total, t_ref, a_ref, wide, sems = refs
    slices, rows, cols = t_hbm.shape
    group = slices // 2
    steps = slices // group

    def load(k):
        part = pl.ds(k * group, group)
        return pltpu.make_async_copy(t_hbm.at[part], t_ref.at[part], sems.at[k])

    first = [
        pltpu.make_async_copy(a_hbm, a_ref, sems.at[slices]),
        pltpu.make_async_copy(c_hbm, c_ref, sems.at[slices + 1]),
    ]
    last = pltpu.make_async_copy(own_hbm, own_ref, sems.at[slices + 2])
    for copy in first + [load(k) for k in range(min(AHEAD, steps))] + [last]:
        copy.start()
    for copy in first:
        copy.wait()
    if other_ref is None:
        block_ref[...] = a_ref[...]
    else:
        here = lax.axis_index("col") == 0
        half = rows // 2
        block_ref[:half, :] = jnp.where(here, a_ref[...], other_ref[...])
        block_ref[half:, :] = jnp.where(here, other_ref[...], a_ref[...])
    rank = block_ref.shape[1]
    a = block_ref[...]
    a_t = a.T
    c_t = c_ref[...].T
    for k in range(slices):
        wide[k] = jnp.broadcast_to(c_t[:, k : k + 1], wide.shape[1:])
    a_pair = split(a_t)
    both = jnp.concatenate(a_pair, axis=1)
    gram = dot3(a_pair, split(a))
    gram_ref[...] = gram
    total[:, :cols] = jnp.zeros((rank, cols), F32)
    if width == rank:
        total[:, cols:] = gram
    else:
        mine = lax.axis_index("col")
        for part in range(rank // width):

            @pl.when(mine == part)
            def _():
                total[:, cols:] = gram[:, part * width : (part + 1) * width]

    @pl.loop(0, steps)
    def _(step):
        load(step).wait()

        @pl.when(step + AHEAD < steps)
        def _():
            load(step + AHEAD).start()

        mul = functools.partial(jnp.dot, preferred_element_type=F32)
        slabs, scales = [], []
        for i in range(group):
            k = step * group + i
            high, low = split(t_ref[k])
            here = pl.ds(pl.multiple_of(k * rows, rows), rows)
            high_ref[here, :] = high
            low_ref[here, :] = low
            slab = mul(both, jnp.concatenate([high, high], axis=0)) + mul(
                both, jnp.concatenate([low, low], axis=0)
            )
            slab_ref[k] = slab
            slabs.append(slab)
            scales.append(wide[k])
        lanes = wide.shape[2]
        for at in range(0, cols, lanes):
            total[:, at : at + lanes] += sum(
                scale * slab[:, at : at + lanes] for scale, slab in zip(scales, slabs)
            )

    last.wait()
    if len(pay) == 1:
        pay[0][...] = total[...]
    else:
        for ref, starts in zip(pay, block_rows(n_line, rank_rows)):
            for d, start in enumerate(starts):
                ref[d * rank_rows : (d + 1) * rank_rows, :] = total[pl.ds(start, rank_rows), :]


def put_ranks(slab_ref, ref, starts, count, high_ref, low_ref, sums_ref):
    for d, start in enumerate(starts):
        block = ref[d * count : (d + 1) * count, :]
        here = pl.ds(start, count)
        high_ref[here, :], low_ref[here, :] = split(block)
        sums_ref[here, :] = jnp.concatenate(
            [
                jnp.sum(slab_ref[k, here, :] * block, axis=1, keepdims=True)
                for k in range(slab_ref.shape[0])
            ],
            axis=1,
        )


def near_kernel(n_line, rank_rows, slab_ref, *refs):
    *bufs, high_ref, low_ref, sums_ref = refs
    for ref, starts in zip(bufs, block_rows(n_line, rank_rows)):
        put_ranks(slab_ref, ref, starts, rank_rows, high_ref, low_ref, sums_ref)


def ranks_kernel(n_line, rank_rows, slab_ref, c_ref, gram_ref, buf_ref, *refs):
    *sofar, high_ref, low_ref, cross_ref, out_ref, sums_ref = refs
    if sofar:
        for ref, out in zip(sofar, (high_ref, low_ref, sums_ref)):
            out[...] = ref[...]
        starts, count = block_rows(n_line, rank_rows)[3], rank_rows
    else:
        starts, count = [0], buf_ref.shape[0]
    put_ranks(slab_ref, buf_ref, starts, count, high_ref, low_ref, sums_ref)
    bt = (high_ref[...], low_ref[...])
    cross = dot3(bt, bt, NT)
    cross_ref[...] = cross
    out_ref[...] = dot3(split(c_ref[...]), split(gram_ref[...] * cross)) - sums_ref[...].T


def rows_kernel(halves, high_ref, low_ref, bt_high, bt_low, a_ref, c_ref, cross_ref, keep_ref, send_ref=None):
    rows, rank = a_ref.shape
    slices = c_ref.shape[0]
    bt = (bt_high[...], bt_low[...])
    total = None
    for k in range(0, slices, 2):
        here = pl.ds(k * rows, 2 * rows)
        contracted = dot3((high_ref[here, :], low_ref[here, :]), bt, NT)
        part = c_ref[k : k + 1, :] * contracted[:rows] + c_ref[k + 1 : k + 2, :] * contracted[rows:]
        total = part if total is None else total + part
    gram_c = dot3(split(c_ref[...].T), split(c_ref[...]))
    grad = dot3(split(a_ref[...]), split(cross_ref[...] * gram_c)) - total
    if not halves:
        keep_ref[...] = grad
        return
    half = rows // 2
    mine = lax.axis_index("col")

    @pl.when(mine == 0)
    def _():
        keep_ref[...] = grad[:half]
        send_ref[...] = grad[half:]

    @pl.when(mine == 1)
    def _():
        keep_ref[...] = grad[half:]
        send_ref[...] = grad[:half]


def sum_kernel(a_ref, b_ref, out_ref):
    out_ref[...] = a_ref[...] + b_ref[...]


def last_kernel(pair, halves, *refs):
    gram_refs, refs = refs[: 1 + halves], refs[1 + halves :]
    c_ref, m_ref, high_ref, low_ref, *refs = refs
    if pair:
        keep_ref, back_ref, *parts, out_ref, a_out, c_out = refs
        a_out[...] = keep_ref[...] + back_ref[...]
        c_out[...] = sum(ref[...] for ref in parts[1:]) + parts[0][...]
    else:
        (out_ref,) = refs
    rank_rows = m_ref.shape[0]
    pieces = [ref[...] for ref in gram_refs]
    if halves:
        here = lax.axis_index("col") == 0
        pieces = [jnp.where(here, *pieces), jnp.where(here, *pieces[::-1])]
    gram_rows = jnp.concatenate(pieces, axis=1)
    c = c_ref[...]
    chosen = lax.axis_index("row") * rank_rows
    rank = c.shape[1]
    pick = lax.broadcasted_iota(jnp.int32, (rank_rows, rank), 1) == (
        chosen + lax.broadcasted_iota(jnp.int32, (rank_rows, rank), 0)
    )
    exact = functools.partial(
        lax.dot_general, precision=lax.Precision.HIGHEST, preferred_element_type=F32
    )
    c_mine = exact(pick.astype(F32), c, NT)
    h_rows = gram_rows * exact(c_mine, c, NN)
    out_ref[...] = dot3(split(h_rows), (high_ref[...], low_ref[...])) - m_ref[...]


def local(n_row, n_col, tensor, factor_a, factor_bt, factor_c):
    slices, rows, cols = tensor.shape
    rank_rows, rank = factor_bt.shape[0], factor_c.shape[1]
    n_line = n_row // 4
    line_rows = n_line * rank_rows
    inside = rank_rows % 16 == 0
    pair = n_col == 2
    width = rank // n_col if (rank // n_col) % 128 == 0 and pair else rank

    def move(x, target):
        return lax.ppermute(
            x,
            ("row", "col"),
            [(r * n_col + c, target(r, c) * n_col + c) for r in range(n_row) for c in range(n_col)],
        )

    def swap(x):
        return lax.ppermute(x, "col", [(0, 1), (1, 0)])

    first = lambda r, c: r ^ (1 + c % 2)
    second = lambda r, c: r ^ (2 - c % 2)

    def call(kernel, name, cost, shapes, scratch=()):
        return pl.pallas_call(
            kernel,
            out_shape=[jax.ShapeDtypeStruct(*x) for x in shapes],
            scratch_shapes=[pltpu.VMEM(x, F32) for x in scratch],
            compiler_params=pltpu.CompilerParams(vmem_limit_bytes=VMEM),
            cost_estimate=pl.CostEstimate(flops=cost, bytes_accessed=0, transcendentals=0),
            name=name,
        )

    tie = lax.optimization_barrier

    if pair:
        a_parts = [factor_a, swap(factor_a)]
    else:
        a_parts = [lax.all_gather(factor_a, "col", axis=0, tiled=True)]
    apart = [lambda r, c, d=d: r ^ (4 * distance(d, n_line, c % 2)) for d in range(n_line)]
    got = [move(factor_bt, apart[d]) for d in range(1, n_line)]

    work = 2 * slices * rows * cols * rank
    pay_rows = [line_rows] * 4 if inside else [rank]
    early = functools.partial(early_kernel, n_line, rank_rows, width)
    if pair:
        kernel = early
    else:
        kernel = lambda t_ref, a_ref, c_ref, b_ref, *refs: early(t_ref, a_ref, c_ref, b_ref, None, *refs)
    fixed = pltpu.with_memory_space_constraint
    hbm = pl.BlockSpec(memory_space=pltpu.HBM)
    vmem = pl.BlockSpec(memory_space=pltpu.VMEM)
    *pay, slabs, high, low, gram, block_a, c_near, own = pl.pallas_call(
        kernel,
        in_specs=[hbm] * 4 + [vmem] * (len(a_parts) - 1),
        out_shape=[jax.ShapeDtypeStruct((n, cols + width), F32) for n in pay_rows]
        + [jax.ShapeDtypeStruct((slices, rank, cols), F32)]
        + [jax.ShapeDtypeStruct((slices * rows, cols), BF16)] * 2
        + [jax.ShapeDtypeStruct(x, F32) for x in ((rank, rank), (rows, rank), (slices, rank), factor_bt.shape)],
        scratch_shapes=[
            pltpu.VMEM((rank, cols + width), F32),
            pltpu.VMEM((slices, rows, cols), F32),
            pltpu.VMEM(a_parts[0].shape, F32),
            pltpu.VMEM((slices, rank, 128), F32),
            pltpu.SemaphoreType.DMA((slices + 3,)),
        ],
        compiler_params=pltpu.CompilerParams(vmem_limit_bytes=EARLY_VMEM),
        cost_estimate=pl.CostEstimate(flops=work, bytes_accessed=0, transcendentals=0),
        name="early",
    )(*(fixed(x, pltpu.HBM) for x in (tensor, a_parts[0], factor_c, factor_bt)), *a_parts[1:])
    if not inside:
        row, parity = lax.axis_index("row"), lax.axis_index("col") % 2
        line, spot, step = row // 4, row % 4, 1 + parity
        lines = jnp.stack([line ^ distance(d, n_line, parity) for d in range(n_line)])
        places = (spot, spot ^ step, spot ^ (3 - step), spot ^ 3)
        blocks = pay[0].reshape(n_line, 4, rank_rows, cols + width)
        pay = [
            jnp.take(jnp.take(blocks, place, axis=1), lines, axis=0).reshape(line_rows, cols + width)
            for place in places
        ]
    pay_own, pay_f, pay_s, pay_fs = pay
    got_f = move(pay_f, first)
    got_fs = move(pay_fs, first)

    own4 = jnp.concatenate([own, *got], axis=0)
    f4 = move(own4, first)
    s4 = move(own4, second)
    f4, s4 = tie((f4, s4))
    fs4 = move(f4, second)
    if inside:
        sofar = call(
            functools.partial(near_kernel, n_line, rank_rows),
            "near",
            WEIGHT * cols * rank * rank,
            [((rank, cols), BF16)] * 2 + [((rank, slices), F32)],
        )(slabs, own4, f4, s4)
        got_fs, _ = tie((got_fs, sofar[2]))
        last_ranks = fs4
    else:
        sofar = []
        table = jnp.concatenate([own4, f4, s4, fs4], axis=0).reshape(n_row, rank_rows, cols)
        index = jnp.argsort(jnp.concatenate([4 * lines + place for place in places]))
        last_ranks = jnp.take(table, index, axis=0).reshape(rank, cols)
    bt_high, bt_low, cross, part_c = call(
        functools.partial(ranks_kernel, n_line, rank_rows),
        "ranks",
        WEIGHT * cols * rank * rank,
        [((rank, cols), BF16)] * 2 + [((rank, rank), F32), ((slices, rank), F32)],
        [(rank, slices)],
    )(slabs, c_near, gram, last_ranks, *sofar)

    got_s = move(pay_s + got_fs, second)

    (mark,) = call(sum_kernel, "mark", WEIGHT * work, [(part_c.shape, F32)])(part_c, part_c)
    part_c = part_c + swap(part_c) if pair else lax.psum(part_c, "col")
    (part_c,) = call(sum_kernel, "sum", WEIGHT * work, [(part_c.shape, F32)])(part_c, move(part_c, second))
    pay_own, _ = tie((pay_own, mark))
    total = pay_own + got_f + got_s
    slots = jnp.split(total, n_line, axis=0)
    total = slots[0]
    for d in range(1, n_line):
        total = total + move(slots[d], apart[d])
    cross, _ = tie((cross, part_c))
    part_c = part_c + move(part_c, first)

    half = rows // 2 if pair else rows
    keep, *send = call(
        functools.partial(rows_kernel, pair),
        "rows",
        work,
        [((half, rank), F32)] * (2 if pair else 1),
    )(high, low, bt_high, bt_low, block_a, c_near, cross)

    part_c = [part_c] + [move(part_c, lambda r, c, d=d: r ^ (4 * d)) for d in reversed(range(1, n_line))]
    gram_rows = total[:, cols:]
    grams = [gram_rows, swap(gram_rows)] if width < rank else [gram_rows]
    operands = [*grams, c_near, total[:, :cols], bt_high, bt_low]
    shapes = [((rank_rows, cols), F32)]
    if pair:
        operands += [keep, swap(send[0]), *part_c]
        shapes += [(keep.shape, F32), (factor_c.shape, F32)]
    grad_bt, *rest = call(
        functools.partial(last_kernel, pair, len(grams) - 1), "last", rank_rows * cols * rank, shapes
    )(*operands)
    if pair:
        return rest[0], grad_bt, rest[1]
    grad_a = lax.psum_scatter(keep, "col", scatter_dimension=0, tiled=True)
    return grad_a, grad_bt, sum(part_c[1:], part_c[0])


def solution(mesh):
    in_specs = (P(None, "row", "col"), P(("row", "col"), None), P("row", "col"), P())
    out_specs = (P(("row", "col"), None), P("row", "col"), P())
    body = functools.partial(local, mesh.shape["row"], mesh.shape["col"])
    return jax.shard_map(body, mesh=mesh, in_specs=in_specs, out_specs=out_specs, check_vma=False)
```

```python
import functools

import jax
import jax.numpy as jnp
from jax import lax
from jax.experimental import pallas as pl
from jax.experimental.pallas import tpu as pltpu
from jax.sharding import PartitionSpec as P

F32 = jnp.float32
BF16 = jnp.bfloat16
NN = (((1,), (0,)), ((), ()))
NT = (((1,), (1,)), ((), ()))
VMEM = 24 * 1024 * 1024
EARLY_VMEM = VMEM
AHEAD = 4
WEIGHT = 200


def split(x):
    high = x.astype(BF16)
    return high, (x - high.astype(F32)).astype(BF16)


def dot3(a, b, dims=NN):
    mul = functools.partial(lax.dot_general, dimension_numbers=dims, preferred_element_type=F32)
    return mul(a[0], b[0]) + (mul(a[0], b[1]) + mul(a[1], b[0]))


def distance(slot, n_line, parity):
    if slot in (0, n_line - 1):
        return min(slot, 1)
    return (slot + 1) ^ parity


def block_rows(n_line, rank_rows):
    row, col = lax.axis_index("row"), lax.axis_index("col")
    line, spot, parity = row // 4, row % 4, col % 2
    step = 1 + parity
    places = (spot, spot ^ step, spot ^ (3 - step), spot ^ 3)
    return [
        [
            pl.multiple_of((4 * (line ^ distance(d, n_line, parity)) + place) * rank_rows, rank_rows)
            for d in range(n_line)
        ]
        for place in places
    ]


def early_kernel(n_line, rank_rows, width, t_hbm, a_hbm, c_hbm, own_hbm, other_ref, *refs):
    *pay, slab_ref, high_ref, low_ref, gram_ref, block_ref, c_ref, own_ref, total, t_ref, a_ref, wide, sems = refs
    slices, rows, cols = t_hbm.shape
    group = slices // 2
    steps = slices // group

    def load(k):
        part = pl.ds(k * group, group)
        return pltpu.make_async_copy(t_hbm.at[part], t_ref.at[part], sems.at[k])

    first = [
        pltpu.make_async_copy(a_hbm, a_ref, sems.at[slices]),
        pltpu.make_async_copy(c_hbm, c_ref, sems.at[slices + 1]),
    ]
    last = pltpu.make_async_copy(own_hbm, own_ref, sems.at[slices + 2])
    for copy in first + [load(k) for k in range(min(AHEAD, steps))] + [last]:
        copy.start()
    for copy in first:
        copy.wait()
    if other_ref is None:
        block_ref[...] = a_ref[...]
    else:
        here = lax.axis_index("col") == 0
        half = rows // 2
        block_ref[:half, :] = jnp.where(here, a_ref[...], other_ref[...])
        block_ref[half:, :] = jnp.where(here, other_ref[...], a_ref[...])
    rank = block_ref.shape[1]
    a = block_ref[...]
    a_t = a.T
    c_t = c_ref[...].T
    for k in range(slices):
        wide[k] = jnp.broadcast_to(c_t[:, k : k + 1], wide.shape[1:])
    a_pair = split(a_t)
    both = jnp.concatenate(a_pair, axis=1)
    gram = dot3(a_pair, split(a))
    gram_ref[...] = gram
    total[:, :cols] = jnp.zeros((rank, cols), F32)
    if width == rank:
        total[:, cols:] = gram
    else:
        mine = lax.axis_index("col")
        for part in range(rank // width):

            @pl.when(mine == part)
            def _():
                total[:, cols:] = gram[:, part * width : (part + 1) * width]

    @pl.loop(0, steps)
    def _(step):
        load(step).wait()

        @pl.when(step + AHEAD < steps)
        def _():
            load(step + AHEAD).start()

        mul = functools.partial(jnp.dot, preferred_element_type=F32)
        slabs, scales = [], []
        for i in range(group):
            k = step * group + i
            high, low = split(t_ref[k])
            here = pl.ds(pl.multiple_of(k * rows, rows), rows)
            high_ref[here, :] = high
            low_ref[here, :] = low
            slab = mul(both, jnp.concatenate([high, high], axis=0)) + mul(
                both, jnp.concatenate([low, low], axis=0)
            )
            slab_ref[k] = slab
            slabs.append(slab)
            scales.append(wide[k])
        lanes = wide.shape[2]
        for at in range(0, cols, lanes):
            total[:, at : at + lanes] += sum(
                scale * slab[:, at : at + lanes] for scale, slab in zip(scales, slabs)
            )

    last.wait()
    if len(pay) == 1:
        pay[0][...] = total[...]
    else:
        for ref, starts in zip(pay, block_rows(n_line, rank_rows)):
            for d, start in enumerate(starts):
                ref[d * rank_rows : (d + 1) * rank_rows, :] = total[pl.ds(start, rank_rows), :]


def put_ranks(slab_ref, ref, starts, count, high_ref, low_ref, sums_ref):
    for d, start in enumerate(starts):
        block = ref[d * count : (d + 1) * count, :]
        here = pl.ds(start, count)
        high_ref[here, :], low_ref[here, :] = split(block)
        sums_ref[here, :] = jnp.concatenate(
            [
                jnp.sum(slab_ref[k, here, :] * block, axis=1, keepdims=True)
                for k in range(slab_ref.shape[0])
            ],
            axis=1,
        )


def near_kernel(n_line, rank_rows, slab_ref, *refs):
    *bufs, high_ref, low_ref, sums_ref = refs
    for ref, starts in zip(bufs, block_rows(n_line, rank_rows)):
        put_ranks(slab_ref, ref, starts, rank_rows, high_ref, low_ref, sums_ref)


def ranks_kernel(n_line, rank_rows, slab_ref, c_ref, gram_ref, buf_ref, *refs):
    *sofar, high_ref, low_ref, cross_ref, out_ref, sums_ref = refs
    if sofar:
        for ref, out in zip(sofar, (high_ref, low_ref, sums_ref)):
            out[...] = ref[...]
        starts, count = block_rows(n_line, rank_rows)[3], rank_rows
    else:
        starts, count = [0], buf_ref.shape[0]
    put_ranks(slab_ref, buf_ref, starts, count, high_ref, low_ref, sums_ref)
    bt = (high_ref[...], low_ref[...])
    cross = dot3(bt, bt, NT)
    cross_ref[...] = cross
    out_ref[...] = dot3(split(c_ref[...]), split(gram_ref[...] * cross)) - sums_ref[...].T


def rows_kernel(halves, high_ref, low_ref, bt_high, bt_low, a_ref, c_ref, cross_ref, keep_ref, send_ref=None):
    rows, rank = a_ref.shape
    slices = c_ref.shape[0]
    bt = (bt_high[...], bt_low[...])
    total = None
    for k in range(0, slices, 2):
        here = pl.ds(k * rows, 2 * rows)
        contracted = dot3((high_ref[here, :], low_ref[here, :]), bt, NT)
        part = c_ref[k : k + 1, :] * contracted[:rows] + c_ref[k + 1 : k + 2, :] * contracted[rows:]
        total = part if total is None else total + part
    gram_c = dot3(split(c_ref[...].T), split(c_ref[...]))
    grad = dot3(split(a_ref[...]), split(cross_ref[...] * gram_c)) - total
    if not halves:
        keep_ref[...] = grad
        return
    half = rows // 2
    mine = lax.axis_index("col")

    @pl.when(mine == 0)
    def _():
        keep_ref[...] = grad[:half]
        send_ref[...] = grad[half:]

    @pl.when(mine == 1)
    def _():
        keep_ref[...] = grad[half:]
        send_ref[...] = grad[:half]


def sum_kernel(a_ref, b_ref, out_ref):
    out_ref[...] = a_ref[...] + b_ref[...]


def last_kernel(pair, halves, *refs):
    gram_refs, refs = refs[: 1 + halves], refs[1 + halves :]
    c_ref, m_ref, high_ref, low_ref, *refs = refs
    if pair:
        keep_ref, back_ref, *parts, out_ref, a_out, c_out = refs
        a_out[...] = keep_ref[...] + back_ref[...]
        c_out[...] = sum(ref[...] for ref in parts[1:]) + parts[0][...]
    else:
        (out_ref,) = refs
    rank_rows = m_ref.shape[0]
    pieces = [ref[...] for ref in gram_refs]
    if halves:
        here = lax.axis_index("col") == 0
        pieces = [jnp.where(here, *pieces), jnp.where(here, *pieces[::-1])]
    gram_rows = jnp.concatenate(pieces, axis=1)
    c = c_ref[...]
    chosen = lax.axis_index("row") * rank_rows
    rank = c.shape[1]
    pick = lax.broadcasted_iota(jnp.int32, (rank_rows, rank), 1) == (
        chosen + lax.broadcasted_iota(jnp.int32, (rank_rows, rank), 0)
    )
    exact = functools.partial(
        lax.dot_general, precision=lax.Precision.HIGHEST, preferred_element_type=F32
    )
    c_mine = exact(pick.astype(F32), c, NT)
    h_rows = gram_rows * exact(c_mine, c, NN)
    out_ref[...] = dot3(split(h_rows), (high_ref[...], low_ref[...])) - m_ref[...]


def local(n_row, n_col, tensor, factor_a, factor_bt, factor_c):
    slices, rows, cols = tensor.shape
    rank_rows, rank = factor_bt.shape[0], factor_c.shape[1]
    n_line = n_row // 4
    line_rows = n_line * rank_rows
    inside = rank_rows % 16 == 0
    pair = n_col == 2
    width = rank // n_col if (rank // n_col) % 128 == 0 and pair else rank

    def move(x, target):
        return lax.ppermute(
            x,
            ("row", "col"),
            [(r * n_col + c, target(r, c) * n_col + c) for r in range(n_row) for c in range(n_col)],
        )

    def swap(x):
        return lax.ppermute(x, "col", [(0, 1), (1, 0)])

    first = lambda r, c: r ^ (1 + c % 2)
    second = lambda r, c: r ^ (2 - c % 2)

    def call(kernel, name, cost, shapes, scratch=()):
        return pl.pallas_call(
            kernel,
            out_shape=[jax.ShapeDtypeStruct(*x) for x in shapes],
            scratch_shapes=[pltpu.VMEM(x, F32) for x in scratch],
            compiler_params=pltpu.CompilerParams(vmem_limit_bytes=VMEM),
            cost_estimate=pl.CostEstimate(flops=cost, bytes_accessed=0, transcendentals=0),
            name=name,
        )

    tie = lax.optimization_barrier

    if pair:
        a_parts = [factor_a, swap(factor_a)]
    else:
        a_parts = [lax.all_gather(factor_a, "col", axis=0, tiled=True)]
    apart = [lambda r, c, d=d: r ^ (4 * distance(d, n_line, c % 2)) for d in range(n_line)]
    got = [move(factor_bt, apart[d]) for d in range(1, n_line)]

    work = 2 * slices * rows * cols * rank
    pay_rows = [line_rows] * 4 if inside else [rank]
    early = functools.partial(early_kernel, n_line, rank_rows, width)
    if pair:
        kernel = early
    else:
        kernel = lambda t_ref, a_ref, c_ref, b_ref, *refs: early(t_ref, a_ref, c_ref, b_ref, None, *refs)
    fixed = pltpu.with_memory_space_constraint
    hbm = pl.BlockSpec(memory_space=pltpu.HBM)
    vmem = pl.BlockSpec(memory_space=pltpu.VMEM)
    *pay, slabs, high, low, gram, block_a, c_near, own = pl.pallas_call(
        kernel,
        in_specs=[hbm] * 4 + [vmem] * (len(a_parts) - 1),
        out_shape=[jax.ShapeDtypeStruct((n, cols + width), F32) for n in pay_rows]
        + [jax.ShapeDtypeStruct((slices, rank, cols), F32)]
        + [jax.ShapeDtypeStruct((slices * rows, cols), BF16)] * 2
        + [jax.ShapeDtypeStruct(x, F32) for x in ((rank, rank), (rows, rank), (slices, rank), factor_bt.shape)],
        scratch_shapes=[
            pltpu.VMEM((rank, cols + width), F32),
            pltpu.VMEM((slices, rows, cols), F32),
            pltpu.VMEM(a_parts[0].shape, F32),
            pltpu.VMEM((slices, rank, 128), F32),
            pltpu.SemaphoreType.DMA((slices + 3,)),
        ],
        compiler_params=pltpu.CompilerParams(vmem_limit_bytes=EARLY_VMEM),
        cost_estimate=pl.CostEstimate(flops=work, bytes_accessed=0, transcendentals=0),
        name="early",
    )(*(fixed(x, pltpu.HBM) for x in (tensor, a_parts[0], factor_c, factor_bt)), *a_parts[1:])
    if not inside:
        row, parity = lax.axis_index("row"), lax.axis_index("col") % 2
        line, spot, step = row // 4, row % 4, 1 + parity
        lines = jnp.stack([line ^ distance(d, n_line, parity) for d in range(n_line)])
        places = (spot, spot ^ step, spot ^ (3 - step), spot ^ 3)
        blocks = pay[0].reshape(n_line, 4, rank_rows, cols + width)
        pay = [
            jnp.take(jnp.take(blocks, place, axis=1), lines, axis=0).reshape(line_rows, cols + width)
            for place in places
        ]
    pay_own, pay_f, pay_s, pay_fs = pay
    got_f = move(pay_f, first)
    got_fs = move(pay_fs, first)

    own4 = jnp.concatenate([own, *got], axis=0)
    f4 = move(own4, first)
    s4 = move(own4, second)
    f4, s4 = tie((f4, s4))
    fs4 = move(f4, second)
    if inside:
        sofar = call(
            functools.partial(near_kernel, n_line, rank_rows),
            "near",
            WEIGHT * cols * rank * rank,
            [((rank, cols), BF16)] * 2 + [((rank, slices), F32)],
        )(slabs, own4, f4, s4)
        got_fs, _ = tie((got_fs, sofar[2]))
        last_ranks = fs4
    else:
        sofar = []
        table = jnp.concatenate([own4, f4, s4, fs4], axis=0).reshape(n_row, rank_rows, cols)
        index = jnp.argsort(jnp.concatenate([4 * lines + place for place in places]))
        last_ranks = jnp.take(table, index, axis=0).reshape(rank, cols)
    bt_high, bt_low, cross, part_c = call(
        functools.partial(ranks_kernel, n_line, rank_rows),
        "ranks",
        WEIGHT * cols * rank * rank,
        [((rank, cols), BF16)] * 2 + [((rank, rank), F32), ((slices, rank), F32)],
        [(rank, slices)],
    )(slabs, c_near, gram, last_ranks, *sofar)

    got_s = move(pay_s + got_fs, second)

    (mark,) = call(sum_kernel, "mark", WEIGHT * work, [(part_c.shape, F32)])(part_c, part_c)
    part_c = part_c + swap(part_c) if pair else lax.psum(part_c, "col")
    (part_c,) = call(sum_kernel, "sum", WEIGHT * work, [(part_c.shape, F32)])(part_c, move(part_c, second))
    pay_own, _ = tie((pay_own, mark))
    total = pay_own + got_f + got_s
    slots = jnp.split(total, n_line, axis=0)
    total = slots[0]
    for d in reversed(range(1, n_line)):
        total = total + move(slots[d], apart[d])
    cross, _ = tie((cross, part_c))
    part_c = part_c + move(part_c, first)

    half = rows // 2 if pair else rows
    keep, *send = call(
        functools.partial(rows_kernel, pair),
        "rows",
        work,
        [((half, rank), F32)] * (2 if pair else 1),
    )(high, low, bt_high, bt_low, block_a, c_near, cross)

    part_c = [part_c] + [move(part_c, lambda r, c, d=d: r ^ (4 * d)) for d in reversed(range(1, n_line))]
    gram_rows = total[:, cols:]
    grams = [gram_rows, swap(gram_rows)] if width < rank else [gram_rows]
    operands = [*grams, c_near, total[:, :cols], bt_high, bt_low]
    shapes = [((rank_rows, cols), F32)]
    if pair:
        operands += [keep, swap(send[0]), *part_c]
        shapes += [(keep.shape, F32), (factor_c.shape, F32)]
    grad_bt, *rest = call(
        functools.partial(last_kernel, pair, len(grams) - 1), "last", rank_rows * cols * rank, shapes
    )(*operands)
    if pair:
        return rest[0], grad_bt, rest[1]
    grad_a = lax.psum_scatter(keep, "col", scatter_dimension=0, tiled=True)
    return grad_a, grad_bt, sum(part_c[1:], part_c[0])


def solution(mesh):
    in_specs = (P(None, "row", "col"), P(("row", "col"), None), P("row", "col"), P())
    out_specs = (P(("row", "col"), None), P("row", "col"), P())
    body = functools.partial(local, mesh.shape["row"], mesh.shape["col"])
    return jax.shard_map(body, mesh=mesh, in_specs=in_specs, out_specs=out_specs, check_vma=False)
```

```python
import functools

import jax
import jax.numpy as jnp
from jax import lax
from jax.experimental import pallas as pl
from jax.experimental.pallas import tpu as pltpu
from jax.sharding import PartitionSpec as P

F32 = jnp.float32
BF16 = jnp.bfloat16
NN = (((1,), (0,)), ((), ()))
NT = (((1,), (1,)), ((), ()))
VMEM = 24 * 1024 * 1024
EARLY_VMEM = VMEM
AHEAD = 4
WEIGHT = 200


def split(x):
    high = x.astype(BF16)
    return high, (x - high.astype(F32)).astype(BF16)


def dot3(a, b, dims=NN):
    mul = functools.partial(lax.dot_general, dimension_numbers=dims, preferred_element_type=F32)
    return mul(a[0], b[0]) + (mul(a[0], b[1]) + mul(a[1], b[0]))


def distance(slot, n_line, parity):
    if slot in (0, n_line - 1):
        return min(slot, 1)
    return (slot + 1) ^ parity


def block_rows(n_line, rank_rows):
    row, col = lax.axis_index("row"), lax.axis_index("col")
    line, spot, parity = row // 4, row % 4, col % 2
    step = 1 + parity
    places = (spot, spot ^ step, spot ^ (3 - step), spot ^ 3)
    return [
        [
            pl.multiple_of((4 * (line ^ distance(d, n_line, parity)) + place) * rank_rows, rank_rows)
            for d in range(n_line)
        ]
        for place in places
    ]


def early_kernel(n_line, rank_rows, width, t_hbm, a_hbm, c_hbm, own_hbm, other_ref, *refs):
    *pay, slab_ref, high_ref, low_ref, gram_ref, block_ref, c_ref, own_ref, rows_ref, total, t_ref, a_ref, wide, sems = refs
    slices, rows, cols = t_hbm.shape
    group = slices // 2
    steps = slices // group

    def load(k):
        part = pl.ds(k * group, group)
        return pltpu.make_async_copy(t_hbm.at[part], t_ref.at[part], sems.at[k])

    first = [
        pltpu.make_async_copy(a_hbm, a_ref, sems.at[slices]),
        pltpu.make_async_copy(c_hbm, c_ref, sems.at[slices + 1]),
    ]
    last = pltpu.make_async_copy(own_hbm, own_ref, sems.at[slices + 2])
    for copy in first + [load(k) for k in range(min(AHEAD, steps))] + [last]:
        copy.start()
    for copy in first:
        copy.wait()
    if other_ref is None:
        block_ref[...] = a_ref[...]
    else:
        here = lax.axis_index("col") == 0
        half = rows // 2
        block_ref[:half, :] = jnp.where(here, a_ref[...], other_ref[...])
        block_ref[half:, :] = jnp.where(here, other_ref[...], a_ref[...])
    rank = block_ref.shape[1]
    a = block_ref[...]
    a_t = a.T
    c_t = c_ref[...].T
    for k in range(slices):
        wide[k] = jnp.broadcast_to(c_t[:, k : k + 1], wide.shape[1:])
    a_pair = split(a_t)
    both = jnp.concatenate(a_pair, axis=1)
    gram = dot3(a_pair, split(a))
    gram_ref[...] = gram
    total[:, :cols] = jnp.zeros((rank, cols), F32)
    if width == rank:
        total[:, cols:] = gram
    else:
        mine = lax.axis_index("col")
        for part in range(rank // width):

            @pl.when(mine == part)
            def _():
                total[:, cols:] = gram[:, part * width : (part + 1) * width]

    @pl.loop(0, steps)
    def _(step):
        load(step).wait()

        @pl.when(step + AHEAD < steps)
        def _():
            load(step + AHEAD).start()

        mul = functools.partial(jnp.dot, preferred_element_type=F32)
        slabs, scales = [], []
        for i in range(group):
            k = step * group + i
            high, low = split(t_ref[k])
            here = pl.ds(pl.multiple_of(k * rows, rows), rows)
            high_ref[here, :] = high
            low_ref[here, :] = low
            slab = mul(both, jnp.concatenate([high, high], axis=0)) + mul(
                both, jnp.concatenate([low, low], axis=0)
            )
            slab_ref[k] = slab
            slabs.append(slab)
            scales.append(wide[k])
        lanes = wide.shape[2]
        for at in range(0, cols, lanes):
            total[:, at : at + lanes] += sum(
                scale * slab[:, at : at + lanes] for scale, slab in zip(scales, slabs)
            )

    c = c_ref[...]
    chosen = lax.axis_index("row") * rank_rows
    pick = lax.broadcasted_iota(jnp.int32, (rank_rows, rank), 1) == (
        chosen + lax.broadcasted_iota(jnp.int32, (rank_rows, rank), 0)
    )
    exact = functools.partial(
        lax.dot_general, precision=lax.Precision.HIGHEST, preferred_element_type=F32
    )
    rows_ref[...] = exact(exact(pick.astype(F32), c, NT), c, NN)
    last.wait()
    if len(pay) == 1:
        pay[0][...] = total[...]
    else:
        for ref, starts in zip(pay, block_rows(n_line, rank_rows)):
            for d, start in enumerate(starts):
                ref[d * rank_rows : (d + 1) * rank_rows, :] = total[pl.ds(start, rank_rows), :]


def put_ranks(slab_ref, ref, starts, count, high_ref, low_ref, sums_ref):
    for d, start in enumerate(starts):
        block = ref[d * count : (d + 1) * count, :]
        here = pl.ds(start, count)
        high_ref[here, :], low_ref[here, :] = split(block)
        sums_ref[here, :] = jnp.concatenate(
            [
                jnp.sum(slab_ref[k, here, :] * block, axis=1, keepdims=True)
                for k in range(slab_ref.shape[0])
            ],
            axis=1,
        )


def near_kernel(n_line, rank_rows, slab_ref, *refs):
    *bufs, high_ref, low_ref, sums_ref = refs
    for ref, starts in zip(bufs, block_rows(n_line, rank_rows)):
        put_ranks(slab_ref, ref, starts, rank_rows, high_ref, low_ref, sums_ref)


def ranks_kernel(n_line, rank_rows, slab_ref, c_ref, gram_ref, buf_ref, *refs):
    *sofar, high_ref, low_ref, cross_ref, out_ref, sums_ref = refs
    if sofar:
        for ref, out in zip(sofar, (high_ref, low_ref, sums_ref)):
            out[...] = ref[...]
        starts, count = block_rows(n_line, rank_rows)[3], rank_rows
    else:
        starts, count = [0], buf_ref.shape[0]
    put_ranks(slab_ref, buf_ref, starts, count, high_ref, low_ref, sums_ref)
    bt = (high_ref[...], low_ref[...])
    cross = dot3(bt, bt, NT)
    cross_ref[...] = cross
    out_ref[...] = dot3(split(c_ref[...]), split(gram_ref[...] * cross)) - sums_ref[...].T


def rows_kernel(halves, high_ref, low_ref, bt_high, bt_low, a_ref, c_ref, cross_ref, keep_ref, send_ref=None):
    rows, rank = a_ref.shape
    slices = c_ref.shape[0]
    bt = (bt_high[...], bt_low[...])
    total = None
    for k in range(0, slices, 2):
        here = pl.ds(k * rows, 2 * rows)
        contracted = dot3((high_ref[here, :], low_ref[here, :]), bt, NT)
        part = c_ref[k : k + 1, :] * contracted[:rows] + c_ref[k + 1 : k + 2, :] * contracted[rows:]
        total = part if total is None else total + part
    gram_c = dot3(split(c_ref[...].T), split(c_ref[...]))
    grad = dot3(split(a_ref[...]), split(cross_ref[...] * gram_c)) - total
    if not halves:
        keep_ref[...] = grad
        return
    half = rows // 2
    mine = lax.axis_index("col")

    @pl.when(mine == 0)
    def _():
        keep_ref[...] = grad[:half]
        send_ref[...] = grad[half:]

    @pl.when(mine == 1)
    def _():
        keep_ref[...] = grad[half:]
        send_ref[...] = grad[:half]


def sum_kernel(a_ref, b_ref, out_ref):
    out_ref[...] = a_ref[...] + b_ref[...]


def last_kernel(pair, halves, *refs):
    gram_refs, refs = refs[: 1 + halves], refs[1 + halves :]
    c_ref, m_ref, high_ref, low_ref, *refs = refs
    if pair:
        keep_ref, back_ref, *parts, out_ref, a_out, c_out = refs
        a_out[...] = keep_ref[...] + back_ref[...]
        c_out[...] = sum(ref[...] for ref in parts[1:]) + parts[0][...]
    else:
        (out_ref,) = refs
    rank_rows = m_ref.shape[0]
    pieces = [ref[...] for ref in gram_refs]
    if halves:
        here = lax.axis_index("col") == 0
        pieces = [jnp.where(here, *pieces), jnp.where(here, *pieces[::-1])]
    gram_rows = jnp.concatenate(pieces, axis=1)
    h_rows = gram_rows * c_ref[...]
    out_ref[...] = dot3(split(h_rows), (high_ref[...], low_ref[...])) - m_ref[...]


def local(n_row, n_col, tensor, factor_a, factor_bt, factor_c):
    slices, rows, cols = tensor.shape
    rank_rows, rank = factor_bt.shape[0], factor_c.shape[1]
    n_line = n_row // 4
    line_rows = n_line * rank_rows
    inside = rank_rows % 16 == 0
    pair = n_col == 2
    width = rank // n_col if (rank // n_col) % 128 == 0 and pair else rank

    def move(x, target):
        return lax.ppermute(
            x,
            ("row", "col"),
            [(r * n_col + c, target(r, c) * n_col + c) for r in range(n_row) for c in range(n_col)],
        )

    def swap(x):
        return lax.ppermute(x, "col", [(0, 1), (1, 0)])

    first = lambda r, c: r ^ (1 + c % 2)
    second = lambda r, c: r ^ (2 - c % 2)

    def call(kernel, name, cost, shapes, scratch=()):
        return pl.pallas_call(
            kernel,
            out_shape=[jax.ShapeDtypeStruct(*x) for x in shapes],
            scratch_shapes=[pltpu.VMEM(x, F32) for x in scratch],
            compiler_params=pltpu.CompilerParams(vmem_limit_bytes=VMEM),
            cost_estimate=pl.CostEstimate(flops=cost, bytes_accessed=0, transcendentals=0),
            name=name,
        )

    tie = lax.optimization_barrier

    if pair:
        a_parts = [factor_a, swap(factor_a)]
    else:
        a_parts = [lax.all_gather(factor_a, "col", axis=0, tiled=True)]
    apart = [lambda r, c, d=d: r ^ (4 * distance(d, n_line, c % 2)) for d in range(n_line)]
    got = [move(factor_bt, apart[d]) for d in range(1, n_line)]

    work = 2 * slices * rows * cols * rank
    pay_rows = [line_rows] * 4 if inside else [rank]
    early = functools.partial(early_kernel, n_line, rank_rows, width)
    if pair:
        kernel = early
    else:
        kernel = lambda t_ref, a_ref, c_ref, b_ref, *refs: early(t_ref, a_ref, c_ref, b_ref, None, *refs)
    fixed = pltpu.with_memory_space_constraint
    hbm = pl.BlockSpec(memory_space=pltpu.HBM)
    vmem = pl.BlockSpec(memory_space=pltpu.VMEM)
    *pay, slabs, high, low, gram, block_a, c_near, own, c_rows = pl.pallas_call(
        kernel,
        in_specs=[hbm] * 4 + [vmem] * (len(a_parts) - 1),
        out_shape=[jax.ShapeDtypeStruct((n, cols + width), F32) for n in pay_rows]
        + [jax.ShapeDtypeStruct((slices, rank, cols), F32)]
        + [jax.ShapeDtypeStruct((slices * rows, cols), BF16)] * 2
        + [jax.ShapeDtypeStruct(x, F32) for x in ((rank, rank), (rows, rank), (slices, rank), factor_bt.shape, (rank_rows, rank))],
        scratch_shapes=[
            pltpu.VMEM((rank, cols + width), F32),
            pltpu.VMEM((slices, rows, cols), F32),
            pltpu.VMEM(a_parts[0].shape, F32),
            pltpu.VMEM((slices, rank, 128), F32),
            pltpu.SemaphoreType.DMA((slices + 3,)),
        ],
        compiler_params=pltpu.CompilerParams(vmem_limit_bytes=EARLY_VMEM),
        cost_estimate=pl.CostEstimate(flops=work, bytes_accessed=0, transcendentals=0),
        name="early",
    )(*(fixed(x, pltpu.HBM) for x in (tensor, a_parts[0], factor_c, factor_bt)), *a_parts[1:])
    if not inside:
        row, parity = lax.axis_index("row"), lax.axis_index("col") % 2
        line, spot, step = row // 4, row % 4, 1 + parity
        lines = jnp.stack([line ^ distance(d, n_line, parity) for d in range(n_line)])
        places = (spot, spot ^ step, spot ^ (3 - step), spot ^ 3)
        blocks = pay[0].reshape(n_line, 4, rank_rows, cols + width)
        pay = [
            jnp.take(jnp.take(blocks, place, axis=1), lines, axis=0).reshape(line_rows, cols + width)
            for place in places
        ]
    pay_own, pay_f, pay_s, pay_fs = pay
    got_f = move(pay_f, first)
    got_fs = move(pay_fs, first)

    own4 = jnp.concatenate([own, *got], axis=0)
    f4 = move(own4, first)
    s4 = move(own4, second)
    f4, s4 = tie((f4, s4))
    fs4 = move(f4, second)
    if inside:
        sofar = call(
            functools.partial(near_kernel, n_line, rank_rows),
            "near",
            WEIGHT * cols * rank * rank,
            [((rank, cols), BF16)] * 2 + [((rank, slices), F32)],
        )(slabs, own4, f4, s4)
        got_fs, _ = tie((got_fs, sofar[2]))
        last_ranks = fs4
    else:
        sofar = []
        table = jnp.concatenate([own4, f4, s4, fs4], axis=0).reshape(n_row, rank_rows, cols)
        index = jnp.argsort(jnp.concatenate([4 * lines + place for place in places]))
        last_ranks = jnp.take(table, index, axis=0).reshape(rank, cols)
    bt_high, bt_low, cross, part_c = call(
        functools.partial(ranks_kernel, n_line, rank_rows),
        "ranks",
        WEIGHT * cols * rank * rank,
        [((rank, cols), BF16)] * 2 + [((rank, rank), F32), ((slices, rank), F32)],
        [(rank, slices)],
    )(slabs, c_near, gram, last_ranks, *sofar)

    got_s = move(pay_s + got_fs, second)

    (mark,) = call(sum_kernel, "mark", WEIGHT * work, [(part_c.shape, F32)])(part_c, part_c)
    part_c = part_c + swap(part_c) if pair else lax.psum(part_c, "col")
    (part_c,) = call(sum_kernel, "sum", WEIGHT * work, [(part_c.shape, F32)])(part_c, move(part_c, second))
    pay_own, _ = tie((pay_own, mark))
    total = pay_own + got_f + got_s
    slots = jnp.split(total, n_line, axis=0)
    total = slots[0]
    for d in reversed(range(1, n_line)):
        total = total + move(slots[d], apart[d])
    cross, _ = tie((cross, part_c))
    part_c = part_c + move(part_c, first)

    half = rows // 2 if pair else rows
    keep, *send = call(
        functools.partial(rows_kernel, pair),
        "rows",
        work,
        [((half, rank), F32)] * (2 if pair else 1),
    )(high, low, bt_high, bt_low, block_a, c_near, cross)

    part_c = [part_c] + [move(part_c, lambda r, c, d=d: r ^ (4 * d)) for d in reversed(range(1, n_line))]
    gram_rows = total[:, cols:]
    grams = [gram_rows, swap(gram_rows)] if width < rank else [gram_rows]
    operands = [*grams, c_rows, total[:, :cols], bt_high, bt_low]
    shapes = [((rank_rows, cols), F32)]
    if pair:
        operands += [keep, swap(send[0]), *part_c]
        shapes += [(keep.shape, F32), (factor_c.shape, F32)]
    grad_bt, *rest = call(
        functools.partial(last_kernel, pair, len(grams) - 1), "last", rank_rows * cols * rank, shapes
    )(*operands)
    if pair:
        return rest[0], grad_bt, rest[1]
    grad_a = lax.psum_scatter(keep, "col", scatter_dimension=0, tiled=True)
    return grad_a, grad_bt, sum(part_c[1:], part_c[0])


def solution(mesh):
    in_specs = (P(None, "row", "col"), P(("row", "col"), None), P("row", "col"), P())
    out_specs = (P(("row", "col"), None), P("row", "col"), P())
    body = functools.partial(local, mesh.shape["row"], mesh.shape["col"])
    return jax.shard_map(body, mesh=mesh, in_specs=in_specs, out_specs=out_specs, check_vma=False)
```

```python
import functools

import jax
import jax.numpy as jnp
from jax import lax
from jax.experimental import pallas as pl
from jax.experimental.pallas import tpu as pltpu
from jax.sharding import PartitionSpec as P

F32 = jnp.float32
BF16 = jnp.bfloat16
NN = (((1,), (0,)), ((), ()))
NT = (((1,), (1,)), ((), ()))
VMEM = 24 * 1024 * 1024
EARLY_VMEM = VMEM
AHEAD = 4
WEIGHT = 200


def split(x):
    high = x.astype(BF16)
    return high, (x - high.astype(F32)).astype(BF16)


def dot3(a, b, dims=NN):
    mul = functools.partial(lax.dot_general, dimension_numbers=dims, preferred_element_type=F32)
    return mul(a[0], b[0]) + (mul(a[0], b[1]) + mul(a[1], b[0]))


def distance(slot, n_line, parity):
    if slot in (0, n_line - 1):
        return min(slot, 1)
    return (slot + 1) ^ parity


def block_rows(n_line, rank_rows):
    row, col = lax.axis_index("row"), lax.axis_index("col")
    line, spot, parity = row // 4, row % 4, col % 2
    step = 1 + parity
    places = (spot, spot ^ step, spot ^ (3 - step), spot ^ 3)
    return [
        [
            pl.multiple_of((4 * (line ^ distance(d, n_line, parity)) + place) * rank_rows, rank_rows)
            for d in range(n_line)
        ]
        for place in places
    ]


def early_kernel(n_line, rank_rows, width, t_hbm, a_hbm, c_hbm, own_hbm, other_ref, *refs):
    *pay, slab_ref, high_ref, low_ref, gram_ref, block_ref, c_ref, own_ref, total, t_ref, a_ref, wide, sems = refs
    slices, rows, cols = t_hbm.shape
    group = slices // 2
    steps = slices // group

    def load(k):
        part = pl.ds(k * group, group)
        return pltpu.make_async_copy(t_hbm.at[part], t_ref.at[part], sems.at[k])

    first = [
        pltpu.make_async_copy(a_hbm, a_ref, sems.at[slices]),
        pltpu.make_async_copy(c_hbm, c_ref, sems.at[slices + 1]),
    ]
    last = pltpu.make_async_copy(own_hbm, own_ref, sems.at[slices + 2])
    for copy in first + [load(k) for k in range(min(AHEAD, steps))] + [last]:
        copy.start()
    for copy in first:
        copy.wait()
    if other_ref is None:
        block_ref[...] = a_ref[...]
    else:
        here = lax.axis_index("col") == 0
        half = rows // 2
        block_ref[:half, :] = jnp.where(here, a_ref[...], other_ref[...])
        block_ref[half:, :] = jnp.where(here, other_ref[...], a_ref[...])
    rank = block_ref.shape[1]
    a = block_ref[...]
    a_t = a.T
    c_t = c_ref[...].T
    for k in range(slices):
        wide[k] = jnp.broadcast_to(c_t[:, k : k + 1], wide.shape[1:])
    a_pair = split(a_t)
    both = jnp.concatenate(a_pair, axis=1)
    gram = dot3(a_pair, split(a))
    gram_ref[...] = gram
    total[:, :cols] = jnp.zeros((rank, cols), F32)
    if width == rank:
        total[:, cols:] = gram
    else:
        mine = lax.axis_index("col")
        for part in range(rank // width):

            @pl.when(mine == part)
            def _():
                total[:, cols:] = gram[:, part * width : (part + 1) * width]

    @pl.loop(0, steps)
    def _(step):
        load(step).wait()

        @pl.when(step + AHEAD < steps)
        def _():
            load(step + AHEAD).start()

        mul = functools.partial(jnp.dot, preferred_element_type=F32)
        slabs, scales = [], []
        for i in range(group):
            k = step * group + i
            high, low = split(t_ref[k])
            here = pl.ds(pl.multiple_of(k * rows, rows), rows)
            high_ref[here, :] = high
            low_ref[here, :] = low
            slab = mul(both, jnp.concatenate([high, high], axis=0)) + mul(
                both, jnp.concatenate([low, low], axis=0)
            )
            slab_ref[k] = slab
            slabs.append(slab)
            scales.append(wide[k])
        lanes = wide.shape[2]
        for at in range(0, cols, lanes):
            total[:, at : at + lanes] += sum(
                scale * slab[:, at : at + lanes] for scale, slab in zip(scales, slabs)
            )

    last.wait()
    if len(pay) == 1:
        pay[0][...] = total[...]
    else:
        for ref, starts in zip(pay, block_rows(n_line, rank_rows)):
            for d, start in enumerate(starts):
                ref[d * rank_rows : (d + 1) * rank_rows, :] = total[pl.ds(start, rank_rows), :]


def put_ranks(slab_ref, ref, starts, count, high_ref, low_ref, sums_ref):
    for d, start in enumerate(starts):
        block = ref[d * count : (d + 1) * count, :]
        here = pl.ds(start, count)
        high_ref[here, :], low_ref[here, :] = split(block)
        sums_ref[here, :] = jnp.concatenate(
            [
                jnp.sum(slab_ref[k, here, :] * block, axis=1, keepdims=True)
                for k in range(slab_ref.shape[0])
            ],
            axis=1,
        )


def near_kernel(n_line, rank_rows, slab_ref, *refs):
    *bufs, high_ref, low_ref, sums_ref = refs
    for ref, starts in zip(bufs, block_rows(n_line, rank_rows)):
        put_ranks(slab_ref, ref, starts, rank_rows, high_ref, low_ref, sums_ref)


def ranks_kernel(n_line, rank_rows, slab_ref, c_ref, gram_ref, buf_ref, *refs):
    *sofar, high_ref, low_ref, cross_ref, out_ref, sums_ref = refs
    if sofar:
        for ref, out in zip(sofar, (high_ref, low_ref, sums_ref)):
            out[...] = ref[...]
        starts, count = block_rows(n_line, rank_rows)[3], rank_rows
    else:
        starts, count = [0], buf_ref.shape[0]
    put_ranks(slab_ref, buf_ref, starts, count, high_ref, low_ref, sums_ref)
    bt = (high_ref[...], low_ref[...])
    cross = dot3(bt, bt, NT)
    cross_ref[...] = cross
    out_ref[...] = dot3(split(c_ref[...]), split(gram_ref[...] * cross)) - sums_ref[...].T


def rows_kernel(halves, high_ref, low_ref, bt_high, bt_low, a_ref, c_ref, cross_ref, keep_ref, send_ref=None):
    rows, rank = a_ref.shape
    slices = c_ref.shape[0]
    bt = (bt_high[...], bt_low[...])
    total = None
    for k in range(0, slices, 2):
        here = pl.ds(k * rows, 2 * rows)
        contracted = dot3((high_ref[here, :], low_ref[here, :]), bt, NT)
        part = c_ref[k : k + 1, :] * contracted[:rows] + c_ref[k + 1 : k + 2, :] * contracted[rows:]
        total = part if total is None else total + part
    gram_c = dot3(split(c_ref[...].T), split(c_ref[...]))
    grad = dot3(split(a_ref[...]), split(cross_ref[...] * gram_c)) - total
    if not halves:
        keep_ref[...] = grad
        return
    half = rows // 2
    mine = lax.axis_index("col")

    @pl.when(mine == 0)
    def _():
        keep_ref[...] = grad[:half]
        send_ref[...] = grad[half:]

    @pl.when(mine == 1)
    def _():
        keep_ref[...] = grad[half:]
        send_ref[...] = grad[:half]


def sum_kernel(a_ref, b_ref, out_ref):
    out_ref[...] = a_ref[...] + b_ref[...]


def last_kernel(pair, halves, *refs):
    gram_refs, refs = refs[: 1 + halves], refs[1 + halves :]
    c_ref, m_ref, high_ref, low_ref, *refs = refs
    if pair:
        keep_ref, back_ref, *parts, out_ref, a_out, c_out = refs
        a_out[...] = keep_ref[...] + back_ref[...]
        c_out[...] = sum(ref[...] for ref in parts[1:]) + parts[0][...]
    else:
        (out_ref,) = refs
    rank_rows = m_ref.shape[0]
    pieces = [ref[...] for ref in gram_refs]
    if halves:
        here = lax.axis_index("col") == 0
        pieces = [jnp.where(here, *pieces), jnp.where(here, *pieces[::-1])]
    gram_rows = jnp.concatenate(pieces, axis=1)
    c = c_ref[...]
    chosen = lax.axis_index("row") * rank_rows
    rank = c.shape[1]
    pick = lax.broadcasted_iota(jnp.int32, (rank_rows, rank), 1) == (
        chosen + lax.broadcasted_iota(jnp.int32, (rank_rows, rank), 0)
    )
    exact = functools.partial(
        lax.dot_general, precision=lax.Precision.HIGHEST, preferred_element_type=F32
    )
    c_mine = exact(pick.astype(F32), c, NT)
    h_rows = gram_rows * exact(c_mine, c, NN)
    out_ref[...] = dot3(split(h_rows), (high_ref[...], low_ref[...])) - m_ref[...]


def local(n_row, n_col, tensor, factor_a, factor_bt, factor_c):
    slices, rows, cols = tensor.shape
    rank_rows, rank = factor_bt.shape[0], factor_c.shape[1]
    n_line = n_row // 4
    line_rows = n_line * rank_rows
    inside = rank_rows % 16 == 0
    pair = n_col == 2
    width = rank // n_col if (rank // n_col) % 128 == 0 and pair else rank

    def move(x, target):
        return lax.ppermute(
            x,
            ("row", "col"),
            [(r * n_col + c, target(r, c) * n_col + c) for r in range(n_row) for c in range(n_col)],
        )

    def swap(x):
        return lax.ppermute(x, "col", [(0, 1), (1, 0)])

    first = lambda r, c: r ^ (1 + c % 2)
    second = lambda r, c: r ^ (2 - c % 2)

    def call(kernel, name, cost, shapes, scratch=()):
        return pl.pallas_call(
            kernel,
            out_shape=[jax.ShapeDtypeStruct(*x) for x in shapes],
            scratch_shapes=[pltpu.VMEM(x, F32) for x in scratch],
            compiler_params=pltpu.CompilerParams(vmem_limit_bytes=VMEM),
            cost_estimate=pl.CostEstimate(flops=cost, bytes_accessed=0, transcendentals=0),
            name=name,
        )

    tie = lax.optimization_barrier

    if pair:
        a_parts = [factor_a, swap(factor_a)]
    else:
        a_parts = [lax.all_gather(factor_a, "col", axis=0, tiled=True)]
    apart = [lambda r, c, d=d: r ^ (4 * distance(d, n_line, c % 2)) for d in range(n_line)]
    got = [move(factor_bt, apart[d]) for d in reversed(range(1, n_line))][::-1]

    work = 2 * slices * rows * cols * rank
    pay_rows = [line_rows] * 4 if inside else [rank]
    early = functools.partial(early_kernel, n_line, rank_rows, width)
    if pair:
        kernel = early
    else:
        kernel = lambda t_ref, a_ref, c_ref, b_ref, *refs: early(t_ref, a_ref, c_ref, b_ref, None, *refs)
    fixed = pltpu.with_memory_space_constraint
    hbm = pl.BlockSpec(memory_space=pltpu.HBM)
    vmem = pl.BlockSpec(memory_space=pltpu.VMEM)
    *pay, slabs, high, low, gram, block_a, c_near, own = pl.pallas_call(
        kernel,
        in_specs=[hbm] * 4 + [vmem] * (len(a_parts) - 1),
        out_shape=[jax.ShapeDtypeStruct((n, cols + width), F32) for n in pay_rows]
        + [jax.ShapeDtypeStruct((slices, rank, cols), F32)]
        + [jax.ShapeDtypeStruct((slices * rows, cols), BF16)] * 2
        + [jax.ShapeDtypeStruct(x, F32) for x in ((rank, rank), (rows, rank), (slices, rank), factor_bt.shape)],
        scratch_shapes=[
            pltpu.VMEM((rank, cols + width), F32),
            pltpu.VMEM((slices, rows, cols), F32),
            pltpu.VMEM(a_parts[0].shape, F32),
            pltpu.VMEM((slices, rank, 128), F32),
            pltpu.SemaphoreType.DMA((slices + 3,)),
        ],
        compiler_params=pltpu.CompilerParams(vmem_limit_bytes=EARLY_VMEM),
        cost_estimate=pl.CostEstimate(flops=work, bytes_accessed=0, transcendentals=0),
        name="early",
    )(*(fixed(x, pltpu.HBM) for x in (tensor, a_parts[0], factor_c, factor_bt)), *a_parts[1:])
    if not inside:
        row, parity = lax.axis_index("row"), lax.axis_index("col") % 2
        line, spot, step = row // 4, row % 4, 1 + parity
        lines = jnp.stack([line ^ distance(d, n_line, parity) for d in range(n_line)])
        places = (spot, spot ^ step, spot ^ (3 - step), spot ^ 3)
        blocks = pay[0].reshape(n_line, 4, rank_rows, cols + width)
        pay = [
            jnp.take(jnp.take(blocks, place, axis=1), lines, axis=0).reshape(line_rows, cols + width)
            for place in places
        ]
    pay_own, pay_f, pay_s, pay_fs = pay
    got_f = move(pay_f, first)
    got_fs = move(pay_fs, first)

    own4 = jnp.concatenate([own, *got], axis=0)
    f4 = move(own4, first)
    s4 = move(own4, second)
    f4, s4 = tie((f4, s4))
    fs4 = move(f4, second)
    if inside:
        sofar = call(
            functools.partial(near_kernel, n_line, rank_rows),
            "near",
            WEIGHT * cols * rank * rank,
            [((rank, cols), BF16)] * 2 + [((rank, slices), F32)],
        )(slabs, own4, f4, s4)
        got_fs, _ = tie((got_fs, sofar[2]))
        last_ranks = fs4
    else:
        sofar = []
        table = jnp.concatenate([own4, f4, s4, fs4], axis=0).reshape(n_row, rank_rows, cols)
        index = jnp.argsort(jnp.concatenate([4 * lines + place for place in places]))
        last_ranks = jnp.take(table, index, axis=0).reshape(rank, cols)
    bt_high, bt_low, cross, part_c = call(
        functools.partial(ranks_kernel, n_line, rank_rows),
        "ranks",
        WEIGHT * cols * rank * rank,
        [((rank, cols), BF16)] * 2 + [((rank, rank), F32), ((slices, rank), F32)],
        [(rank, slices)],
    )(slabs, c_near, gram, last_ranks, *sofar)

    got_s = move(pay_s + got_fs, second)

    (mark,) = call(sum_kernel, "mark", WEIGHT * work, [(part_c.shape, F32)])(part_c, part_c)
    part_c = part_c + swap(part_c) if pair else lax.psum(part_c, "col")
    (part_c,) = call(sum_kernel, "sum", WEIGHT * work, [(part_c.shape, F32)])(part_c, move(part_c, second))
    pay_own, _ = tie((pay_own, mark))
    total = pay_own + got_f + got_s
    slots = jnp.split(total, n_line, axis=0)
    total = slots[0]
    for d in reversed(range(1, n_line)):
        total = total + move(slots[d], apart[d])
    cross, _ = tie((cross, part_c))
    part_c = part_c + move(part_c, first)

    half = rows // 2 if pair else rows
    keep, *send = call(
        functools.partial(rows_kernel, pair),
        "rows",
        work,
        [((half, rank), F32)] * (2 if pair else 1),
    )(high, low, bt_high, bt_low, block_a, c_near, cross)

    part_c = [part_c] + [move(part_c, lambda r, c, d=d: r ^ (4 * d)) for d in reversed(range(1, n_line))]
    gram_rows = total[:, cols:]
    grams = [gram_rows, swap(gram_rows)] if width < rank else [gram_rows]
    operands = [*grams, c_near, total[:, :cols], bt_high, bt_low]
    shapes = [((rank_rows, cols), F32)]
    if pair:
        operands += [keep, swap(send[0]), *part_c]
        shapes += [(keep.shape, F32), (factor_c.shape, F32)]
    grad_bt, *rest = call(
        functools.partial(last_kernel, pair, len(grams) - 1), "last", rank_rows * cols * rank, shapes
    )(*operands)
    if pair:
        return rest[0], grad_bt, rest[1]
    grad_a = lax.psum_scatter(keep, "col", scatter_dimension=0, tiled=True)
    return grad_a, grad_bt, sum(part_c[1:], part_c[0])


def solution(mesh):
    in_specs = (P(None, "row", "col"), P(("row", "col"), None), P("row", "col"), P())
    out_specs = (P(("row", "col"), None), P("row", "col"), P())
    body = functools.partial(local, mesh.shape["row"], mesh.shape["col"])
    return jax.shard_map(body, mesh=mesh, in_specs=in_specs, out_specs=out_specs, check_vma=False)
```
